256 devices in a mesh: rep: 4 (over z_hi, core), fsdp: 64 (over z_lo, x, y).
Axes of the slice: x: 4, y: 4, z: 8 (z_hi: 2, z_lo: 4; z = z_hi * 4 + z_lo), core: 2. Of those that a mesh axis runs over, the one named last changes fastest.
Arguments:
- grad_parts: bfloat16 [4, 16384, 8192], P('rep', 'fsdp'), may hold values from -6 to 6
- adam_m: float32 [4, 256, 8192], P('rep', 'fsdp'), may hold values from -16 to 16
- adam_v: float32 [4, 256, 8192], P('rep', 'fsdp'), may hold values from 1 to 10
- params_inner: float32 [4, 256, 8192], P('rep', 'fsdp'), may hold values from -3 to 3
- snapshot: float32 [256, 8192], P('fsdp'), may hold values from -1.5 to 1.5
- momentum: float32 [256, 8192], P('fsdp'), may hold values from -0.3 to 0.3
Outputs:
- adam_m_next: float32 [4, 256, 8192], P('rep', 'fsdp')
- adam_v_next: float32 [4, 256, 8192], P('rep', 'fsdp')
- params_next: float32 [256, 8192], P('fsdp', 'rep')
- momentum_next: float32 [256, 8192], P('fsdp', 'rep')
- weights: bfloat16 [256, 8192], replicated
The draws below stay inside these ranges and needn't reach their ends.
All inputs are finite; a program needn't handle non-finite values. Where the reference program divides by a largest or mean magnitude, that divisor is 1e-20 or more.
Results may differ from the reference program's by a relative error of at most 0.0095.
Values may be sent and summed in bfloat16 or wider, within the bound.
A program may use at most 64 MiB of HBM per device.

```python
import math
import jax
import jax.numpy as jnp
from jax import lax

D = 8192
ROWS = 256
BLOCK = 128
REPS = 4
NBLK = 2
N_FSDP = 64


def sign_field(key):
    base = jax.random.fold_in(key, 101)
    return jnp.where(jax.random.uniform(base, (ROWS, D), jnp.float32) < 0.5, -1.0, 1.0).astype(jnp.float32)


def coherent_size(key):
    base = jax.random.fold_in(key, 103)
    return jax.random.uniform(base, (REPS, ROWS, D), jnp.float32, 0.25, 0.5)


def snapshot_field(key):
    base = jax.random.fold_in(key, 11)
    return jnp.clip(0.25 * jax.random.normal(base, (ROWS, D), jnp.float32), -1.5, 1.5)


def drift_field(key):
    signs = sign_field(key)[None]
    base = jax.random.fold_in(key, 23)
    keys = jax.random.split(base, 5)
    position = (jnp.arange(ROWS) % BLOCK).astype(jnp.float32) / BLOCK
    ramp = jnp.exp(math.log(10.0) * position)[None, :, None]
    rough = jax.random.uniform(keys[0], (1, ROWS, 1), jnp.float32, 0.75, 1.5)
    offset = jax.random.randint(keys[4], (), 0, REPS)
    replica_ids = jnp.arange(REPS, dtype=jnp.int32)[:, None]
    block_ids = (jnp.arange(ROWS, dtype=jnp.int32) // BLOCK)[None, :]
    quiet = (replica_ids + block_ids + offset) % REPS == 0
    level = jnp.where(quiet, 0.06, 1.0).astype(jnp.float32)[:, :, None]
    column_scale = jnp.exp(jax.random.uniform(keys[1], (1, 1, D), jnp.float32, 0.0, math.log(10.0)))
    cell = jax.random.uniform(keys[2], (REPS, ROWS, D), jnp.float32, 0.7, 1.0)
    return 0.005 * level * ramp * rough * column_scale * cell * signs


def draw_grad_parts(key, part):
    signal = sign_field(key)[None] * coherent_size(key)
    key = jax.random.fold_in(key, 5)
    noise = jnp.clip(jax.random.normal(key, (REPS, N_FSDP, ROWS, D), jnp.float32), -5.0, 5.0)
    return (signal[:, None] + noise).reshape(REPS, N_FSDP * ROWS, D).astype(jnp.bfloat16)


def draw_adam_m(key, part):
    signal = sign_field(key)[None] * coherent_size(key)
    key = jax.random.fold_in(key, 7)
    share = jax.random.uniform(key, (REPS, ROWS, D), jnp.float32, 0.3, 0.5)
    return N_FSDP * signal * share


def draw_snapshot(key, part):
    return snapshot_field(key)


def draw_params_inner(key, part):
    return snapshot_field(key)[None] - drift_field(key)


def level_of(rng, dims, cuts, low, high):
    def one(axis_at, parts):
        draws = jax.random.uniform(jax.random.fold_in(jax.random.fold_in(rng, 6), axis_at), (parts,), jnp.float32, low / len(cuts), high / len(cuts))
        return jnp.repeat(jnp.exp(draws), dims[axis_at] // parts).reshape((-1,) + (1,) * (len(dims) - axis_at - 1))

    factor_of = one(*cuts[0])
    for cut in cuts[1:]:
        factor_of = factor_of * one(*cut)
    return factor_of


def normal_values(key, dims, scale, limit, pieces=(), kind=jnp.bfloat16):
    drawn = scale * jax.random.normal(key, dims, jnp.float32)
    if pieces:
        drawn = drawn * level_of(key, dims, pieces, -0.22, 0.18)
    return jnp.clip(drawn, -limit, limit).astype(kind)


def setup_inputs(seed: int = 0) -> dict:
    streams_of = jax.random.split(jax.random.key(seed), 7)
    grad_parts = draw_grad_parts(jax.random.fold_in(streams_of[6], 71), 0)
    adam_m = draw_adam_m(jax.random.fold_in(streams_of[6], 71), 0)
    adam_v = jnp.clip(jnp.exp(math.log(10.0) - 2.3025851 * jax.random.uniform(streams_of[2], (REPS, ROWS, D), jnp.float32) ** level_of(streams_of[2], (REPS, ROWS, D), ((0, 4), (1, 64)), -0.2, 0.2)), 1.0, 10.0)
    params_inner = draw_params_inner(jax.random.fold_in(streams_of[6], 71), 0)
    snapshot = draw_snapshot(jax.random.fold_in(streams_of[6], 71), 0)
    momentum = normal_values(streams_of[5], (ROWS, D), 0.05, 0.3, ((0, 64),), jnp.float32)
    return dict(grad_parts=grad_parts, adam_m=adam_m, adam_v=adam_v, params_inner=params_inner, snapshot=snapshot, momentum=momentum)


def reference(grad_parts, adam_m, adam_v, params_inner, snapshot, momentum):
    slabs = grad_parts.reshape(REPS, N_FSDP, ROWS, D)

    def add_slab(which, running):
        piece = lax.dynamic_slice_in_dim(slabs, which, 1, 1)[:, 0]
        return running + piece.astype(jnp.float32)
    gradient = lax.fori_loop(0, N_FSDP, add_slab, jnp.zeros((REPS, ROWS, D), jnp.float32))
    adam_m_next = 0.9 * adam_m + 0.1 * gradient
    adam_v_next = 0.95 * adam_v + 0.05 * gradient * gradient
    update = adam_m_next / (jnp.sqrt(adam_v_next) + 1e-08)
    inner_params = params_inner - 0.02 * (update + 0.1 * params_inner)
    pseudo = snapshot[None] - inner_params
    blocked = pseudo.reshape(REPS, NBLK, BLOCK, D)
    peaks = lax.optimization_barrier(jnp.max(jnp.abs(blocked), axis=(2, 3)))
    factor = 0.5 / jnp.maximum(peaks, 0.5)
    clipped = (blocked * factor[:, :, None, None]).reshape(REPS, ROWS, D)
    averaged = lax.optimization_barrier(jnp.sum(clipped, axis=0)) / REPS
    momentum_next = 0.9 * momentum + averaged
    params_next = snapshot - 0.7 * (averaged + 0.9 * momentum_next)
    weights = params_next.astype(jnp.bfloat16)
    return (adam_m_next, adam_v_next, params_next, momentum_next, weights)
```

```python
import functools

import jax
import jax.numpy as jnp
from jax import lax
from jax.experimental import pallas as pl
from jax.experimental.pallas import tpu as pltpu
from jax.sharding import PartitionSpec as P

D = 8192
K = 2
NR = 2 * K
W = D // NR
CW = W // 4
HW = CW // 2
NSEM = 200
F32 = jnp.float32
BF16 = jnp.bfloat16


def mo(v, m=128):
    return pl.multiple_of(v, m)


class Ring:
    def __init__(self, net, i, to_next, to_prev, raw, own, land, acc):
        self.net, self.i = net, i
        self.to_next, self.to_prev = to_next, to_prev
        self.raw, self.own, self.land, self.acc = raw, own, land, acc

    def start(self):
        i, net = self.i, self.net
        nxt, prv, far = (i + 1) % 4, (i + 3) % 4, (i + 2) % 4
        self.a = [
            net.send(self.raw(far, 0), self.land.at[0, 0], self.to_next),
            net.send(self.raw(far, 1), self.land.at[1, 0], self.to_prev),
        ]
        self.b = [
            net.send(self.raw(nxt, 1), self.land.at[0, 1], self.to_next),
            net.send(self.raw(prv, 0), self.land.at[1, 1], self.to_prev),
        ]

    def forward(self):
        i, net = self.i, self.net
        nxt, prv = (i + 1) % 4, (i + 3) % 4
        self.a[0].wait_recv()
        add(self.acc.at[0], [self.own(nxt, 0), self.land.at[0, 0]])
        c0 = net.send(self.acc.at[0], self.land.at[0, 2], self.to_next)
        self.a[1].wait_recv()
        add(self.acc.at[1], [self.own(prv, 1), self.land.at[1, 0]])
        c1 = net.send(self.acc.at[1], self.land.at[1, 2], self.to_prev)
        self.c = [c0, c1]

    def wait(self):
        for cp in self.b + self.c:
            cp.wait_recv()

    def terms(self, hh):
        land = self.land
        if hh == 0:
            return [self.own(self.i, 0), land.at[0, 2], land.at[1, 1]]
        return [self.own(self.i, 1), land.at[0, 1], land.at[1, 2]]


def add(dst, srcs):
    shape = dst.shape
    if len(shape) == 4:

        def body(j, _):
            dst[:, j] = functools.reduce(
                jnp.add, [s[:, j].astype(F32) for s in srcs]
            ).astype(BF16)
            return 0

        lax.fori_loop(0, shape[1], body, 0)
    else:

        def body(j, _):
            at = pl.ds(mo(j * 512, 512), 512)
            dst[:, :, at] = functools.reduce(
                jnp.add, [s[:, :, at].astype(F32) for s in srcs]
            ).astype(BF16)
            return 0

        lax.fori_loop(0, shape[2] // 512, body, 0)


class Net:
    def __init__(self, ss, rs):
        self.ss, self.rs, self.n = ss, rs, 0
        self.sent = []

    def send(self, src, dst, dev):
        n = self.n
        self.n += 1
        assert n < NSEM
        cp = pltpu.make_async_remote_copy(
            src, dst, self.ss.at[n], self.rs.at[n], device_id=dev
        )
        cp.start()
        self.sent.append(cp)
        return cp


def rows4(v, b):
    return v[4 * b : 4 * b + 4]


def kernel(
    grad, m_ref, v_ref, p_ref, snap, mom,
    m_out, v_out, pn_out, mn_out, w_out,
    G, LX1, LY1, AX1, AY1, SX1, SY1, L2, A2, M3, R3, Gs, PK, P1, P2, Pq, E, T, RT, Wb,
    ss, rs, ls,
):
    rep, f = lax.axis_index("rep"), lax.axis_index("fsdp")
    h, c = rep // 2, rep % 2
    z, x, y = f // 16, (f // 4) % 4, f % 4
    zp = z + 1 - 2 * (z % 2)
    Z = 4 * h + z

    def dev(h=h, c=c, z=z, x=x, y=y):
        return (2 * h + c, 16 * z + 4 * x + y)

    loc = []
    for r in range(NR):
        at = pl.ds(r * W, W)
        cp = pltpu.make_async_copy(grad.at[:, :, :, at], G.at[:, :, :, at], ls.at[r])
        cp.start()
        loc.append(cp)

    peers = [dev(x=(x + a) % 4, y=(y + b) % 4) for a in range(4) for b in range(4) if a or b]
    peers += [dev(z=(z + a) % 4, y=(y + b) % 4) for a in range(1, 4) for b in range(4)]
    peers += [dev(h=1 - h, z=(z + a) % 4) for a in range(4)]
    peers += [dev(h=hh, c=1 - c, z=zz) for hh in (h, 1 - h) for zz in (z, zp)]
    bar = pltpu.get_barrier_semaphore()
    for d in peers:
        pl.semaphore_signal(bar, 1, device_id=d)
    pl.semaphore_wait(bar, len(peers))

    net = Net(ss, rs)
    xn, xp = dev(x=(x + 1) % 4), dev(x=(x + 3) % 4)
    yn, yp = dev(y=(y + 1) % 4), dev(y=(y + 3) % 4)

    def first(r):
        k = r // 2
        if r % 2 == 0:

            def chunk(src, j, hh):
                return src.at[pl.ds(2 * hh, 2), j, :, pl.ds(r * W, W)]

            return Ring(
                net, x, xn, xp, functools.partial(chunk, grad), functools.partial(chunk, G),
                LX1.at[k], AX1.at[k],
            )

        def chunk(src, j, hh):
            return src.at[pl.ds(2 * hh, 2), :, :, pl.ds(mo(r * W + j * CW), CW)]

        return Ring(
            net, y, yn, yp, functools.partial(chunk, grad), functools.partial(chunk, G),
            LY1.at[k], AY1.at[k],
        )

    def second(r):
        k = r // 2
        if r % 2 == 0:

            def chunk(j, hh):
                return SX1.at[k].at[pl.ds(2 * hh, 2), :, pl.ds(mo(j * CW), CW)]

            return Ring(net, y, yn, yp, chunk, chunk, L2.at[r], A2.at[r])

        def chunk(j, hh):
            return SY1.at[k].at[pl.ds(2 * hh, 2), j]

        return Ring(net, x, xn, xp, chunk, chunk, L2.at[r], A2.at[r])

    one = [first(r) for r in range(NR)]
    two = [second(r) for r in range(NR)]

    def finish_first(k):
        for r in (2 * k, 2 * k + 1):
            one[r].wait()
            dst = (SX1 if r % 2 == 0 else SY1).at[k]
            for hh in range(2):
                add(dst.at[pl.ds(2 * hh, 2)], one[r].terms(hh))
        for r in (2 * k, 2 * k + 1):
            two[r].start()

    def finish_second(k):
        rings = two[2 * k], two[2 * k + 1]
        for ring in rings:
            ring.wait()
        for zz in range(4):
            halves = []
            for ring in rings:
                s = functools.reduce(
                    jnp.add, [t[zz % 2].astype(F32) for t in ring.terms(zz // 2)]
                )
                halves += [s[:, :HW], s[:, HW:]]
            for yy in range(4):
                M3[k, zz, yy] = jnp.concatenate([rows4(s, yy) for s in halves], 0).astype(BF16)
        return [
            net.send(
                M3.at[k, (z + dz) % 4, (y + dy) % 4],
                R3.at[k, dz, dy],
                dev(z=(z + dz) % 4, y=(y + dy) % 4),
            )
            for dz in (2, 1, 3, 0)
            for dy in range(4)
            if dz or dy
        ]

    one[0].start()
    one[1].start()
    one[2].start()
    one[3].start()
    for cp in loc:
        cp.wait()
    one[0].forward()
    one[1].forward()
    finish_first(0)
    one[2].forward()
    one[3].forward()
    two[0].forward()
    two[1].forward()
    third = finish_second(0)
    finish_first(1)
    two[2].forward()
    two[3].forward()
    third += finish_second(1)
    for cp in third:
        cp.wait_recv()

    for k in range(K):
        for dy in range(4):
            g = None
            for dz in range(4):
                t = (R3[k, dz, dy] if dz or dy else M3[k, z, y]).astype(F32)
                g = t if g is None else g + t
            ys = (y + 4 - dy) % 4
            for s in range(2):
                for t in range(2):
                    at = pl.ds(mo((2 * k + s) * W + ys * CW + t * HW), HW)
                    Gs[:, at] = rows4(g, 2 * s + t)

    top = None
    for q in range(4):
        parts = []
        for t in range(4):
            at = pl.ds(q * 2048 + t * 512, 512)
            g, params = Gs[:, at], p_ref[:, at]
            m_next = 0.9 * m_ref[:, at] + 0.1 * g
            v_next = 0.95 * v_ref[:, at] + 0.05 * g * g
            m_out[:, at] = m_next
            v_out[:, at] = v_next
            inner = params - 0.02 * (m_next / (jnp.sqrt(v_next) + 1e-8) + 0.1 * params)
            pseudo = snap[:, at] - inner
            parts.append(pseudo)
            size = jnp.abs(pseudo)
            top = size if top is None else jnp.maximum(top, size)
        Pq[q] = jnp.concatenate(parts, 0).astype(BF16)
    tile = functools.reduce(jnp.maximum, [top[:, 128 * i : 128 * i + 128] for i in range(4)])
    PK[0] = jnp.concatenate([tile, tile], 0)

    got = [
        net.send(PK.at[0], P1.at[4 * a + b], dev(x=(x + a) % 4, y=(y + b) % 4))
        for a in range(4)
        for b in range(4)
        if a or b
    ]

    def flip(dr):
        return (1 - h if dr // 2 else h), (1 - c if dr % 2 else c)

    sent_e = []
    for dr in (3, 2, 1):
        h2, c2 = flip(dr)
        sent_e.append(net.send(Pq.at[2 * h2 + c2], E.at[dr], dev(h=h2, c=c2)))
    peak = PK[0]
    for cp in got:
        cp.wait_recv()
    for i in range(1, 16):
        peak = jnp.maximum(peak, P1[i])
    PK[1] = peak
    got = []
    for dr in (3, 2, 1, 0):
        h2, c2 = flip(dr)
        for e in (1, 0):
            if dr or e:
                got.append(
                    net.send(PK.at[1], P2.at[e, dr], dev(h=h2, c=c2, z=zp if e else z))
                )
    for cp in got + sent_e:
        cp.wait_recv()
    total = None
    for dr in range(4):
        high = jnp.maximum(P2[0, dr] if dr else peak, P2[1, dr])
        high = jnp.max(high, axis=(0, 1), keepdims=True)
        factor = 0.5 / jnp.maximum(high, 0.5)
        term = (E[dr] if dr else Pq[rep]).astype(F32) * factor
        total = term if total is None else total + term
    averaged = total / 4
    new = []
    for t in range(4):
        avg = rows4(averaged, t)
        at = pl.ds(mo(rep * 2048 + t * 512), 512)
        m_new = 0.9 * mom[:, at] + avg
        p_new = snap[:, at] - 0.7 * (avg + 0.9 * m_new)
        mn_out[:, pl.ds(t * 512, 512)] = m_new
        pn_out[:, pl.ds(t * 512, 512)] = p_new
        new.append(p_new)
    new = jnp.concatenate(new, 1)
    for yy in range(4):
        pieces = [
            new[:, p * 1024 + yy * 256 + t * 128 : p * 1024 + yy * 256 + t * 128 + 128]
            for p in range(2)
            for t in range(2)
        ]
        T[yy] = jnp.concatenate(pieces, 0).astype(BF16)
    got = [
        net.send(T.at[(y + d) % 4], RT.at[y], dev(y=(y + d) % 4)) for d in (2, 1, 3)
    ]
    RT[y] = T[y]
    for cp in got:
        cp.wait_recv()
    for p in range(2):
        for t in range(2):
            b = 2 * p + t
            Wb[p, :, pl.ds(t * 128, 128)] = jnp.concatenate(
                [rows4(RT[ys].astype(F32), b) for ys in range(4)], 0
            ).astype(BF16)

    def small(p):
        return w_out.at[z, x, :, pl.ds(mo((2 * h + c) * 2048 + p * 1024 + y * 256), 256)]

    for p in range(2):
        cp = pltpu.make_async_copy(Wb.at[p], small(p), ls.at[p])
        cp.start()
        loc[p] = cp
    got = []
    for d in (4, 3, 5, 2, 6, 1, 7):
        Z2 = (Z + d) % 8
        for p in range(2):
            got.append(net.send(Wb.at[p], small(p), dev(h=Z2 // 4, z=Z2 % 4)))
    for p in range(2):
        loc[p].wait()
    for cp in got:
        cp.wait_recv()
    got = []
    for d in (2, 1, 3):
        for p, to in ((0, dev(y=(y + d) % 4)), (1, dev(x=(x + d) % 4))):
            for hh in range(2):
                blk = w_out.at[
                    :, x, :, pl.ds(mo((2 * hh + c) * 2048 + p * 1024 + y * 256), 256)
                ]
                got.append(net.send(blk, blk, to))
    for cp in got:
        cp.wait_recv()

    def large(p, i, hh):
        if p == 0:
            return w_out.at[:, i, :, pl.ds(mo((2 * hh + c) * 2048), 1024)]
        return w_out.at[:, :, :, pl.ds(mo((2 * hh + c) * 2048 + 1024 + i * 256), 256)]

    ways = ((x, xn, xp), (y, yn, yp))
    near = []
    for hh in range(2):
        for p, (i, nx, pv) in enumerate(ways):
            right = net.send(large(p, i, hh), large(p, i, hh), nx)
            left = net.send(large(p, i, 1 - hh), large(p, i, 1 - hh), pv)
            near.append((p, hh, right, left))
    sib = dev(c=1 - c)
    swaps = []

    def swap(p, i, hh):
        swaps.append(net.send(large(p, i, hh), large(p, i, hh), sib))

    for p, (i, _, _) in enumerate(ways):
        for hh in range(2):
            swap(p, i, hh)
    far = []
    for p, hh, right, left in near:
        i, nx, pv = ways[p]
        right.wait_recv()
        prv, nxt = (i + 3) % 4, (i + 1) % 4
        if hh == 0:
            far.append((p, 0, net.send(large(p, prv, 0), large(p, prv, 0), nx)))
        swap(p, prv, hh)
        left.wait_recv()
        if hh == 0:
            far.append((p, 1, net.send(large(p, nxt, 1), large(p, nxt, 1), pv)))
        swap(p, nxt, 1 - hh)
    for p, hh, cp in far:
        cp.wait_recv()
        swap(p, (ways[p][0] + 2) % 4, hh)
    for cp in swaps:
        cp.wait_recv()
    for cp in net.sent:
        cp.wait_send()


def local(grad_parts, adam_m, adam_v, params_inner, snapshot, momentum):
    vmem = pl.BlockSpec(memory_space=pltpu.VMEM)
    hbm = pl.BlockSpec(memory_space=pl.ANY)
    V = pltpu.VMEM
    m, v, pn, mn, w = pl.pallas_call(
        kernel,
        out_shape=(
            jax.ShapeDtypeStruct((4, D), F32),
            jax.ShapeDtypeStruct((4, D), F32),
            jax.ShapeDtypeStruct((4, 2048), F32),
            jax.ShapeDtypeStruct((4, 2048), F32),
            jax.ShapeDtypeStruct((4, 4, 16, D), BF16),
        ),
        in_specs=[hbm] + [vmem] * 5,
        out_specs=(vmem, vmem, vmem, vmem, hbm),
        scratch_shapes=[
            V((4, 4, 16, D), BF16),
            V((K, 2, 3, 2, 16, W), BF16),
            V((K, 2, 3, 2, 4, 16, CW), BF16),
            V((K, 2, 2, 16, W), BF16),
            V((K, 2, 2, 4, 16, CW), BF16),
            V((K, 4, 16, W), BF16),
            V((K, 4, 4, 16, CW), BF16),
            V((NR, 2, 3, 2, 16, CW), BF16),
            V((NR, 2, 2, 16, CW), BF16),
            V((K, 4, 4, 16, HW), BF16),
            V((K, 4, 4, 16, HW), BF16),
            V((4, D), F32),
            V((2, 8, 128), F32),
            V((16, 8, 128), F32),
            V((2, 4, 8, 128), F32),
            V((4, 16, 512), BF16),
            V((4, 16, 512), BF16),
            V((4, 16, 128), BF16),
            V((4, 16, 128), BF16),
            V((2, 16, 256), BF16),
            pltpu.SemaphoreType.DMA((NSEM,)),
            pltpu.SemaphoreType.DMA((NSEM,)),
            pltpu.SemaphoreType.DMA((8,)),
        ],
        compiler_params=pltpu.CompilerParams(
            collective_id=0, has_side_effects=True, vmem_limit_bytes=40 * 2**20
        ),
        name="outer_step",
    )(
        grad_parts.reshape(4, 4, 16, D),
        adam_m[0],
        adam_v[0],
        params_inner[0],
        snapshot,
        momentum,
    )
    return m[None], v[None], pn, mn, w.reshape(256, D)


def solution(mesh):
    rows = P("rep", "fsdp", None)
    flat = P("fsdp", None)
    return jax.shard_map(
        local,
        mesh=mesh,
        in_specs=(rows, rows, rows, rows, flat, flat),
        out_specs=(rows, rows, P("fsdp", "rep"), P("fsdp", "rep"), P()),
        check_vma=False,
    )
```

```python
import functools

import jax
import jax.numpy as jnp
from jax import lax
from jax.experimental import pallas as pl
from jax.experimental.pallas import tpu as pltpu
from jax.sharding import PartitionSpec as P

D = 8192
K = 2
NR = 2 * K
W = D // NR
CW = W // 4
HW = CW // 2
NSEM = 200
F32 = jnp.float32
BF16 = jnp.bfloat16


def mo(v, m=128):
    return pl.multiple_of(v, m)


class Ring:
    def __init__(self, net, i, to_next, to_prev, raw, own, land, acc):
        self.net, self.i = net, i
        self.to_next, self.to_prev = to_next, to_prev
        self.raw, self.own, self.land, self.acc = raw, own, land, acc

    def start(self):
        i, net = self.i, self.net
        nxt, prv, far = (i + 1) % 4, (i + 3) % 4, (i + 2) % 4
        self.a = [
            net.send(self.raw(far, 0), self.land.at[0, 0], self.to_next),
            net.send(self.raw(far, 1), self.land.at[1, 0], self.to_prev),
        ]
        self.b = [
            net.send(self.raw(nxt, 1), self.land.at[0, 1], self.to_next),
            net.send(self.raw(prv, 0), self.land.at[1, 1], self.to_prev),
        ]

    def forward(self):
        i, net = self.i, self.net
        nxt, prv = (i + 1) % 4, (i + 3) % 4
        self.a[0].wait_recv()
        add(self.acc.at[0], [self.own(nxt, 0), self.land.at[0, 0]])
        c0 = net.send(self.acc.at[0], self.land.at[0, 2], self.to_next)
        self.a[1].wait_recv()
        add(self.acc.at[1], [self.own(prv, 1), self.land.at[1, 0]])
        c1 = net.send(self.acc.at[1], self.land.at[1, 2], self.to_prev)
        self.c = [c0, c1]

    def wait(self):
        for cp in self.b + self.c:
            cp.wait_recv()

    def terms(self, hh):
        land = self.land
        if hh == 0:
            return [self.own(self.i, 0), land.at[0, 2], land.at[1, 1]]
        return [self.own(self.i, 1), land.at[0, 1], land.at[1, 2]]


class Direct(Ring):
    def __init__(self, net, i, to, raw, land):
        self.net, self.i, self.to, self.own, self.land = net, i, to, raw, land

    def start(self):
        self.b = [
            self.net.send(self.own((self.i + d) % 4, hh), self.land.at[hh, d - 1], self.to[d - 1])
            for d in (2, 1, 3)
            for hh in range(2)
        ]
        self.c = []

    def forward(self):
        pass

    def terms(self, hh):
        return [self.own(self.i, hh)] + [self.land.at[hh, d] for d in range(3)]


def add(dst, srcs):
    shape = dst.shape
    if len(shape) == 4:

        def body(j, _):
            dst[:, j] = functools.reduce(
                jnp.add, [s[:, j].astype(F32) for s in srcs]
            ).astype(BF16)
            return 0

        lax.fori_loop(0, shape[1], body, 0)
    else:

        def body(j, _):
            at = pl.ds(mo(j * 512, 512), 512)
            dst[:, :, at] = functools.reduce(
                jnp.add, [s[:, :, at].astype(F32) for s in srcs]
            ).astype(BF16)
            return 0

        lax.fori_loop(0, shape[2] // 512, body, 0)


class Net:
    def __init__(self, ss, rs):
        self.ss, self.rs, self.n = ss, rs, 0
        self.sent = []

    def send(self, src, dst, dev):
        n = self.n
        self.n += 1
        assert n < NSEM
        cp = pltpu.make_async_remote_copy(
            src, dst, self.ss.at[n], self.rs.at[n], device_id=dev
        )
        cp.start()
        self.sent.append(cp)
        return cp


def rows4(v, b):
    return v[4 * b : 4 * b + 4]


def kernel(
    grad, m_in, v_in, p_in, snap_in, mom_in,
    m_out, v_out, pn_out, mn_out, w_out,
    m_ref, v_ref, p_ref, snap, mom, G, LX1, LY1, AX1, AY1, SX1, SY1, L2, A2, M3, R3, Gs, PK, P1, P2, Pq, E, T, RT, Wb,
    ss, rs, ls, bs,
):
    rep, f = lax.axis_index("rep"), lax.axis_index("fsdp")
    h, c = rep // 2, rep % 2
    z, x, y = f // 16, (f // 4) % 4, f % 4
    zp = z + 1 - 2 * (z % 2)
    Z = 4 * h + z

    def dev(h=h, c=c, z=z, x=x, y=y):
        return (2 * h + c, 16 * z + 4 * x + y)

    loc = []
    for r in range(NR):
        at = pl.ds(r * W, W)
        cp = pltpu.make_async_copy(grad.at[:, :, :, at], G.at[:, :, :, at], ls.at[r])
        cp.start()
        loc.append(cp)

    held = []
    for n, (src, dst) in enumerate(
        ((m_in, m_ref), (v_in, v_ref), (p_in, p_ref), (snap_in, snap), (mom_in, mom))
    ):
        cp = pltpu.make_async_copy(src, dst, ls.at[NR + n])
        cp.start()
        held.append(cp)

    xn, xp = dev(x=(x + 1) % 4), dev(x=(x + 3) % 4)
    yn, yp = dev(y=(y + 1) % 4), dev(y=(y + 3) % 4)
    sib = dev(c=1 - c)
    Zn, Zp = (Z + 1) % 8, (Z + 7) % 8
    line = [dev(h=Zn // 4, z=Zn % 4), dev(h=Zp // 4, z=Zp % 4), sib]
    bar = pltpu.get_barrier_semaphore()
    for d in [xn, xp, yn, yp] + line:
        pl.semaphore_signal(bar, 1, device_id=d)
    pl.semaphore_wait(bar, 7)

    def ahead(n):
        for d in line:
            pl.semaphore_signal(bs.at[n], 1, device_id=d)
        pl.semaphore_wait(bs.at[n], 3)

    net = Net(ss, rs)

    def first(r):
        k = r // 2
        if r % 2 == 0:

            def chunk(src, j, hh):
                return src.at[pl.ds(2 * hh, 2), j, :, pl.ds(r * W, W)]

            return Ring(
                net, x, xn, xp, functools.partial(chunk, grad), functools.partial(chunk, G),
                LX1.at[k], AX1.at[k],
            )

        def chunk(src, j, hh):
            return src.at[pl.ds(2 * hh, 2), :, :, pl.ds(mo(r * W + j * CW), CW)]

        return Ring(
            net, y, yn, yp, functools.partial(chunk, grad), functools.partial(chunk, G),
            LY1.at[k], AY1.at[k],
        )

    def second(r):
        k = r // 2
        if r % 2 == 0:

            def chunk(j, hh):
                return SX1.at[k].at[pl.ds(2 * hh, 2), :, pl.ds(mo(j * CW), CW)]

            if k == K - 1:
                to = [dev(y=(y + d) % 4) for d in (1, 2, 3)]
                return Direct(net, y, to, chunk, L2.at[r])
            return Ring(net, y, yn, yp, chunk, chunk, L2.at[r], A2.at[r])

        def chunk(j, hh):
            return SY1.at[k].at[pl.ds(2 * hh, 2), j]

        if k == K - 1:
            to = [dev(x=(x + d) % 4) for d in (1, 2, 3)]
            return Direct(net, x, to, chunk, L2.at[r])
        return Ring(net, x, xn, xp, chunk, chunk, L2.at[r], A2.at[r])

    one = [first(r) for r in range(NR)]
    two = [second(r) for r in range(NR)]

    def finish_first(k):
        for r in (2 * k, 2 * k + 1):
            one[r].wait()
            dst = (SX1 if r % 2 == 0 else SY1).at[k]
            for hh in range(2):
                add(dst.at[pl.ds(2 * hh, 2)], one[r].terms(hh))
        for r in (2 * k, 2 * k + 1):
            two[r].start()

    def finish_second(k):
        rings = two[2 * k], two[2 * k + 1]
        for ring in rings:
            ring.wait()
        for zz in range(4):
            halves = []
            for ring in rings:
                s = functools.reduce(
                    jnp.add, [t[zz % 2].astype(F32) for t in ring.terms(zz // 2)]
                )
                halves += [s[:, :HW], s[:, HW:]]
            for yy in range(4):
                M3[k, zz, yy] = jnp.concatenate([rows4(s, yy) for s in halves], 0).astype(BF16)
        return [
            net.send(
                M3.at[k, (z + dz) % 4, (y + dy) % 4],
                R3.at[k, dz, dy],
                dev(z=(z + dz) % 4, y=(y + dy) % 4),
            )
            for dz in (2, 1, 3, 0)
            for dy in range(4)
            if dz or dy
        ]

    one[0].start()
    one[1].start()
    one[2].start()
    one[3].start()
    for n in range(4):
        ahead(n)
    for cp in loc:
        cp.wait()
    one[0].forward()
    one[1].forward()
    one[2].forward()
    one[3].forward()
    finish_first(0)
    finish_first(1)
    two[0].forward()
    two[1].forward()
    third = finish_second(0)
    two[2].forward()
    two[3].forward()
    third += finish_second(1)
    for cp in third:
        cp.wait_recv()
    for k in range(K):
        for dy in range(4):
            g = None
            for dz in range(4):
                t = (R3[k, dz, dy] if dz or dy else M3[k, z, y]).astype(F32)
                g = t if g is None else g + t
            ys = (y + 4 - dy) % 4
            for s in range(2):
                for t in range(2):
                    at = pl.ds(mo((2 * k + s) * W + ys * CW + t * HW), HW)
                    Gs[:, at] = rows4(g, 2 * s + t)

    for cp in held:
        cp.wait()
    top = None
    for q in range(4):
        parts = []
        for t in range(4):
            at = pl.ds(q * 2048 + t * 512, 512)
            g, params = Gs[:, at], p_ref[:, at]
            m_next = 0.9 * m_ref[:, at] + 0.1 * g
            v_next = 0.95 * v_ref[:, at] + 0.05 * g * g
            m_out[:, at] = m_next
            v_out[:, at] = v_next
            inner = params - 0.02 * (m_next / (jnp.sqrt(v_next) + 1e-8) + 0.1 * params)
            pseudo = snap[:, at] - inner
            parts.append(pseudo)
            size = jnp.abs(pseudo)
            top = size if top is None else jnp.maximum(top, size)
        Pq[q] = jnp.concatenate(parts, 0).astype(BF16)
    tile = functools.reduce(jnp.maximum, [top[:, 128 * i : 128 * i + 128] for i in range(4)])
    PK[0] = jnp.concatenate([tile, tile], 0)

    got = [
        net.send(PK.at[0], P1.at[4 * a + b], dev(x=(x + a) % 4, y=(y + b) % 4))
        for a in range(4)
        for b in range(4)
        if a or b
    ]

    def flip(dr):
        return (1 - h if dr // 2 else h), (1 - c if dr % 2 else c)

    sent_e = []
    for dr in (3, 2, 1):
        h2, c2 = flip(dr)
        sent_e.append(net.send(Pq.at[2 * h2 + c2], E.at[dr], dev(h=h2, c=c2)))
    peak = PK[0]
    for cp in got:
        cp.wait_recv()
    for i in range(1, 16):
        peak = jnp.maximum(peak, P1[i])
    PK[1] = peak
    got = []
    for dr in (3, 2, 1, 0):
        h2, c2 = flip(dr)
        for e in (1, 0):
            if dr or e:
                got.append(
                    net.send(PK.at[1], P2.at[e, dr], dev(h=h2, c=c2, z=zp if e else z))
                )
    for cp in got + sent_e:
        cp.wait_recv()
    total = None
    for dr in range(4):
        high = jnp.maximum(P2[0, dr] if dr else peak, P2[1, dr])
        high = jnp.max(high, axis=(0, 1), keepdims=True)
        factor = 0.5 / jnp.maximum(high, 0.5)
        term = (E[dr] if dr else Pq[rep]).astype(F32) * factor
        total = term if total is None else total + term
    averaged = total / 4
    new = []
    for t in range(4):
        avg = rows4(averaged, t)
        at = pl.ds(mo(rep * 2048 + t * 512), 512)
        m_new = 0.9 * mom[:, at] + avg
        p_new = snap[:, at] - 0.7 * (avg + 0.9 * m_new)
        mn_out[:, pl.ds(t * 512, 512)] = m_new
        pn_out[:, pl.ds(t * 512, 512)] = p_new
        new.append(p_new)
    new = jnp.concatenate(new, 1)
    for yy in range(4):
        pieces = [
            new[:, p * 1024 + yy * 256 + t * 128 : p * 1024 + yy * 256 + t * 128 + 128]
            for p in range(2)
            for t in range(2)
        ]
        T[yy] = jnp.concatenate(pieces, 0).astype(BF16)
    got = [
        net.send(T.at[(y + d) % 4], RT.at[y], dev(y=(y + d) % 4)) for d in (2, 1, 3)
    ]
    RT[y] = T[y]
    for cp in got:
        cp.wait_recv()
    for p in range(2):
        for t in range(2):
            b = 2 * p + t
            Wb[p, :, pl.ds(t * 128, 128)] = jnp.concatenate(
                [rows4(RT[ys].astype(F32), b) for ys in range(4)], 0
            ).astype(BF16)

    def small(p):
        return w_out.at[z, x, :, pl.ds(mo((2 * h + c) * 2048 + p * 1024 + y * 256), 256)]

    for p in range(2):
        cp = pltpu.make_async_copy(Wb.at[p], small(p), ls.at[p])
        cp.start()
        loc[p] = cp
    got = []
    for d in (4, 3, 5, 2, 6, 1, 7):
        Z2 = (Z + d) % 8
        for p in range(2):
            got.append(net.send(Wb.at[p], small(p), dev(h=Z2 // 4, z=Z2 % 4)))
    for p in range(2):
        loc[p].wait()
    for cp in got:
        cp.wait_recv()
    got = []
    for d in (2, 1, 3):
        for p, to in ((0, dev(y=(y + d) % 4)), (1, dev(x=(x + d) % 4))):
            for hh in range(2):
                blk = w_out.at[
                    :, x, :, pl.ds(mo((2 * hh + c) * 2048 + p * 1024 + y * 256), 256)
                ]
                got.append(net.send(blk, blk, to))
    for cp in got:
        cp.wait_recv()

    def large(p, i, hh):
        if p == 0:
            return w_out.at[:, i, :, pl.ds(mo((2 * hh + c) * 2048), 1024)]
        return w_out.at[:, :, :, pl.ds(mo((2 * hh + c) * 2048 + 1024 + i * 256), 256)]

    ways = ((x, xn, xp), (y, yn, yp))
    near = []
    for hh in range(2):
        for p, (i, nx, pv) in enumerate(ways):
            right = net.send(large(p, i, hh), large(p, i, hh), nx)
            left = net.send(large(p, i, 1 - hh), large(p, i, 1 - hh), pv)
            near.append((p, hh, right, left))
    swaps = []

    def swap(p, i, hh):
        swaps.append(net.send(large(p, i, hh), large(p, i, hh), sib))

    for p, (i, _, _) in enumerate(ways):
        for hh in range(2):
            swap(p, i, hh)
    far = []
    for p, hh, right, left in near:
        i, nx, pv = ways[p]
        right.wait_recv()
        prv, nxt = (i + 3) % 4, (i + 1) % 4
        if hh == 0:
            far.append((p, 0, net.send(large(p, prv, 0), large(p, prv, 0), nx)))
        swap(p, prv, hh)
        left.wait_recv()
        if hh == 0:
            far.append((p, 1, net.send(large(p, nxt, 1), large(p, nxt, 1), pv)))
        swap(p, nxt, 1 - hh)
    for p, hh, cp in far:
        cp.wait_recv()
        swap(p, (ways[p][0] + 2) % 4, hh)
    for cp in swaps:
        cp.wait_recv()
    for cp in net.sent:
        cp.wait_send()


def flush(*refs):
    n = len(refs) // 2
    sems = refs[2 * n]
    cps = [pltpu.make_async_copy(refs[i], refs[n + i], sems.at[i]) for i in range(n)]
    for cp in cps:
        cp.start()
    for cp in cps:
        cp.wait()


def local(grad_parts, adam_m, adam_v, params_inner, snapshot, momentum):
    vmem = pl.BlockSpec(memory_space=pltpu.VMEM)
    hbm = pl.BlockSpec(memory_space=pl.ANY)
    V = pltpu.VMEM
    args = (
        grad_parts.reshape(4, 4, 16, D),
        adam_m[0],
        adam_v[0],
        params_inner[0],
        snapshot,
        momentum,
    )
    outs = pl.pallas_call(
        kernel,
        out_shape=(
            jax.ShapeDtypeStruct((4, D), F32),
            jax.ShapeDtypeStruct((4, D), F32),
            jax.ShapeDtypeStruct((4, 2048), F32),
            jax.ShapeDtypeStruct((4, 2048), F32),
            jax.ShapeDtypeStruct((4, 4, 16, D), BF16),
        ),
        in_specs=[pl.BlockSpec(memory_space=pltpu.HBM)] * 6,
        out_specs=(vmem, vmem, vmem, vmem, hbm),
        scratch_shapes=[
            V((4, D), F32),
            V((4, D), F32),
            V((4, D), F32),
            V((4, D), F32),
            V((4, D), F32),
            V((4, 4, 16, D), BF16),
            V((K, 2, 3, 2, 16, W), BF16),
            V((K, 2, 3, 2, 4, 16, CW), BF16),
            V((K, 2, 2, 16, W), BF16),
            V((K, 2, 2, 4, 16, CW), BF16),
            V((K, 4, 16, W), BF16),
            V((K, 4, 4, 16, CW), BF16),
            V((NR, 2, 3, 2, 16, CW), BF16),
            V((NR, 2, 2, 16, CW), BF16),
            V((K, 4, 4, 16, HW), BF16),
            V((K, 4, 4, 16, HW), BF16),
            V((4, D), F32),
            V((2, 8, 128), F32),
            V((16, 8, 128), F32),
            V((2, 4, 8, 128), F32),
            V((4, 16, 512), BF16),
            V((4, 16, 512), BF16),
            V((4, 16, 128), BF16),
            V((4, 16, 128), BF16),
            V((2, 16, 256), BF16),
            pltpu.SemaphoreType.DMA((NSEM,)),
            pltpu.SemaphoreType.DMA((NSEM,)),
            pltpu.SemaphoreType.DMA((NR + 5,)),
            pltpu.SemaphoreType.REGULAR((4,)),
        ],
        compiler_params=pltpu.CompilerParams(
            collective_id=0, has_side_effects=True, vmem_limit_bytes=40 * 2**20
        ),
        name="outer_step",
    )(*[pltpu.with_memory_space_constraint(a, pltpu.HBM) for a in args])
    m, v, pn, mn, w = pl.pallas_call(
        flush,
        out_shape=tuple(jax.ShapeDtypeStruct(o.shape, o.dtype) for o in outs),
        in_specs=[hbm] * 5,
        out_specs=(hbm,) * 5,
        scratch_shapes=[pltpu.SemaphoreType.DMA((5,))],
        compiler_params=pltpu.CompilerParams(vmem_limit_bytes=2**20),
        name="write_out",
    )(*outs)
    return m[None], v[None], pn, mn, w.reshape(256, D)


def solution(mesh):
    rows = P("rep", "fsdp", None)
    flat = P("fsdp", None)
    return jax.shard_map(
        local,
        mesh=mesh,
        in_specs=(rows, rows, rows, rows, flat, flat),
        out_specs=(rows, rows, P("fsdp", "rep"), P("fsdp", "rep"), P()),
        check_vma=False,
    )
```

```python
import functools

import jax
import jax.numpy as jnp
from jax import lax
from jax.experimental import pallas as pl
from jax.experimental.pallas import tpu as pltpu
from jax.sharding import PartitionSpec as P

D = 8192
K = 2
NR = 2 * K
W = D // NR
CW = W // 4
HW = CW // 2
NSEM = 240
F32 = jnp.float32
BF16 = jnp.bfloat16


def mo(v, m=128):
    return pl.multiple_of(v, m)


class Ring:
    def __init__(self, net, i, to_next, to_prev, raw, own, land, acc):
        self.net, self.i = net, i
        self.to_next, self.to_prev = to_next, to_prev
        self.raw, self.own, self.land, self.acc = raw, own, land, acc

    def start(self):
        self.start_far()
        self.start_near()

    def start_far(self):
        i, net = self.i, self.net
        far = (i + 2) % 4
        self.a = [
            net.send(self.raw(far, 0), self.land.at[0, 0], self.to_next),
            net.send(self.raw(far, 1), self.land.at[1, 0], self.to_prev),
        ]

    def start_near(self):
        i, net = self.i, self.net
        nxt, prv = (i + 1) % 4, (i + 3) % 4
        self.b = [
            net.send(self.raw(nxt, 1), self.land.at[0, 1], self.to_next),
            net.send(self.raw(prv, 0), self.land.at[1, 1], self.to_prev),
        ]

    def forward(self):
        i, net = self.i, self.net
        nxt, prv = (i + 1) % 4, (i + 3) % 4
        self.a[0].wait_recv()
        add(self.acc.at[0], [self.own(nxt, 0), self.land.at[0, 0]])
        c0 = net.send(self.acc.at[0], self.land.at[0, 2], self.to_next)
        self.a[1].wait_recv()
        add(self.acc.at[1], [self.own(prv, 1), self.land.at[1, 0]])
        c1 = net.send(self.acc.at[1], self.land.at[1, 2], self.to_prev)
        self.c = [c0, c1]

    def wait(self):
        for cp in self.b + self.c:
            cp.wait_recv()

    def terms(self, hh):
        land = self.land
        if hh == 0:
            return [self.own(self.i, 0), land.at[0, 2], land.at[1, 1]]
        return [self.own(self.i, 1), land.at[0, 1], land.at[1, 2]]


class Direct(Ring):
    def __init__(self, net, i, to, raw, land):
        self.net, self.i, self.to, self.own, self.land = net, i, to, raw, land

    def start(self):
        self.b = [
            self.net.send(self.own((self.i + d) % 4, hh), self.land.at[hh, d - 1], self.to[d - 1])
            for d in (2, 1, 3)
            for hh in range(2)
        ]
        self.c = []

    def forward(self):
        pass

    def terms(self, hh):
        return [self.own(self.i, hh)] + [self.land.at[hh, d] for d in range(3)]


def add(dst, srcs):
    shape = dst.shape
    if len(shape) == 4:

        def body(j, _):
            dst[:, j] = functools.reduce(
                jnp.add, [s[:, j].astype(F32) for s in srcs]
            ).astype(BF16)
            return 0

        lax.fori_loop(0, shape[1], body, 0)
    else:

        def body(j, _):
            at = pl.ds(mo(j * 512, 512), 512)
            dst[:, :, at] = functools.reduce(
                jnp.add, [s[:, :, at].astype(F32) for s in srcs]
            ).astype(BF16)
            return 0

        lax.fori_loop(0, shape[2] // 512, body, 0)


class Net:
    def __init__(self, ss, rs):
        self.ss, self.rs, self.n = ss, rs, 0
        self.sent = []

    def send(self, src, dst, dev):
        n = self.n
        self.n += 1
        assert n < NSEM
        cp = pltpu.make_async_remote_copy(
            src, dst, self.ss.at[n], self.rs.at[n], device_id=dev
        )
        cp.start()
        self.sent.append(cp)
        return cp


def offsets(yy):
    return [p * 1024 + yy * 256 + t * 128 for p in range(2) for t in range(2)]


def rows4(v, b):
    return v[4 * b : 4 * b + 4]


def kernel(
    grad, m_in, v_in, p_in, snap_in, mom_in,
    m_out, v_out, pn_out, mn_out, w_out,
    m_ref, v_ref, p_ref, snap, mom, G, LX1, LY1, AX1, AY1, SX1, SY1, L2, A2, M3, R3, Gs, PK, P1, P2, Pq, E, X, SM, SX, Wb,
    ss, rs, ls, bs,
):
    rep, f = lax.axis_index("rep"), lax.axis_index("fsdp")
    h, c = rep // 2, rep % 2
    z, x, y = f // 16, (f // 4) % 4, f % 4
    zp = z + 1 - 2 * (z % 2)
    Z = 4 * h + z

    def dev(h=h, c=c, z=z, x=x, y=y):
        return (2 * h + c, 16 * z + 4 * x + y)

    loc = []
    for r in range(NR):
        at = pl.ds(r * W, W)
        cp = pltpu.make_async_copy(grad.at[:, :, :, at], G.at[:, :, :, at], ls.at[r])
        cp.start()
        loc.append(cp)

    held = []
    for n, (src, dst) in enumerate(
        ((m_in, m_ref), (v_in, v_ref), (p_in, p_ref), (snap_in, snap), (mom_in, mom))
    ):
        cp = pltpu.make_async_copy(src, dst, ls.at[NR + n])
        cp.start()
        held.append(cp)

    xn, xp = dev(x=(x + 1) % 4), dev(x=(x + 3) % 4)
    yn, yp = dev(y=(y + 1) % 4), dev(y=(y + 3) % 4)
    sib = dev(c=1 - c)
    Zn, Zp = (Z + 1) % 8, (Z + 7) % 8
    line = [dev(h=Zn // 4, z=Zn % 4), dev(h=Zp // 4, z=Zp % 4), sib]
    bar = pltpu.get_barrier_semaphore()
    for d in [xn, xp, yn, yp] + line:
        pl.semaphore_signal(bar, 1, device_id=d)
    pl.semaphore_wait(bar, 7)

    def ahead(n):
        for d in line:
            pl.semaphore_signal(bs.at[n], 1, device_id=d)
        pl.semaphore_wait(bs.at[n], 3)

    net = Net(ss, rs)

    def first(r):
        k = r // 2
        if r % 2 == 0:

            def chunk(src, j, hh):
                return src.at[pl.ds(2 * hh, 2), j, :, pl.ds(r * W, W)]

            return Ring(
                net, x, xn, xp, functools.partial(chunk, grad), functools.partial(chunk, G),
                LX1.at[k], AX1.at[k],
            )

        def chunk(src, j, hh):
            return src.at[pl.ds(2 * hh, 2), :, :, pl.ds(mo(r * W + j * CW), CW)]

        return Ring(
            net, y, yn, yp, functools.partial(chunk, grad), functools.partial(chunk, G),
            LY1.at[k], AY1.at[k],
        )

    def second(r):
        k = r // 2
        if r % 2 == 0:

            def chunk(j, hh):
                return SX1.at[k].at[pl.ds(2 * hh, 2), :, pl.ds(mo(j * CW), CW)]

            if k == K - 1:
                to = [dev(y=(y + d) % 4) for d in (1, 2, 3)]
                return Direct(net, y, to, chunk, L2.at[r])
            return Ring(net, y, yn, yp, chunk, chunk, L2.at[r], A2.at[r])

        def chunk(j, hh):
            return SY1.at[k].at[pl.ds(2 * hh, 2), j]

        if k == K - 1:
            to = [dev(x=(x + d) % 4) for d in (1, 2, 3)]
            return Direct(net, x, to, chunk, L2.at[r])
        return Ring(net, x, xn, xp, chunk, chunk, L2.at[r], A2.at[r])

    one = [first(r) for r in range(NR)]
    two = [second(r) for r in range(NR)]

    def finish_first(k):
        for r in (2 * k, 2 * k + 1):
            one[r].wait()
            dst = (SX1 if r % 2 == 0 else SY1).at[k]
            for hh in range(2):
                add(dst.at[pl.ds(2 * hh, 2)], one[r].terms(hh))
        for r in (2 * k, 2 * k + 1):
            two[r].start()

    def finish_second(k):
        rings = two[2 * k], two[2 * k + 1]
        for ring in rings:
            ring.wait()
        for zz in range(4):
            halves = []
            for ring in rings:
                s = functools.reduce(
                    jnp.add, [t[zz % 2].astype(F32) for t in ring.terms(zz // 2)]
                )
                halves += [s[:, :HW], s[:, HW:]]
            for yy in range(4):
                M3[k, zz, yy] = jnp.concatenate([rows4(s, yy) for s in halves], 0).astype(BF16)
        return [
            net.send(
                M3.at[k, (z + dz) % 4, (y + dy) % 4],
                R3.at[k, dz, dy],
                dev(z=(z + dz) % 4, y=(y + dy) % 4),
            )
            for dz in (2, 1, 3, 0)
            for dy in range(4)
            if dz or dy
        ]

    one[0].start()
    one[1].start()
    one[2].start_far()
    one[3].start_far()
    for n in range(4):
        ahead(n)
    for cp in loc:
        cp.wait()
    one[0].forward()
    one[1].forward()
    one[2].start_near()
    one[3].start_near()
    finish_first(0)
    one[2].forward()
    one[3].forward()
    two[0].forward()
    two[1].forward()
    finish_first(1)
    third = finish_second(0)
    for cp in held:
        cp.wait()
    for n, ref in enumerate((snap, mom)):
        for yy in range(4):
            SM[yy, n] = jnp.concatenate(
                [ref[:, pl.ds(mo(rep * 2048 + o), 128)] for o in offsets(yy)], 0
            )
    sm = [net.send(SM.at[(y + d) % 4], SX.at[y], dev(y=(y + d) % 4)) for d in (2, 1, 3)]
    SX[y] = SM[y]
    two[2].forward()
    two[3].forward()
    third += finish_second(1)
    for cp in third:
        cp.wait_recv()
    for k in range(K):
        for dy in range(4):
            g = None
            for dz in range(4):
                t = (R3[k, dz, dy] if dz or dy else M3[k, z, y]).astype(F32)
                g = t if g is None else g + t
            ys = (y + 4 - dy) % 4
            for s in range(2):
                for t in range(2):
                    at = pl.ds(mo((2 * k + s) * W + ys * CW + t * HW), HW)
                    Gs[:, at] = rows4(g, 2 * s + t)

    top = None
    for q in range(4):
        parts = []
        for t in range(4):
            at = pl.ds(q * 2048 + t * 512, 512)
            g, params = Gs[:, at], p_ref[:, at]
            m_next = 0.9 * m_ref[:, at] + 0.1 * g
            v_next = 0.95 * v_ref[:, at] + 0.05 * g * g
            m_out[:, at] = m_next
            v_out[:, at] = v_next
            inner = params - 0.02 * (m_next / (jnp.sqrt(v_next) + 1e-8) + 0.1 * params)
            pseudo = snap[:, at] - inner
            parts.append(pseudo)
            size = jnp.abs(pseudo)
            top = size if top is None else jnp.maximum(top, size)
        wide = jnp.concatenate(parts, 1)
        for yy in range(4):
            Pq[q, yy] = jnp.concatenate([wide[:, o : o + 128] for o in offsets(yy)], 0).astype(BF16)
    tile = functools.reduce(jnp.maximum, [top[:, 128 * i : 128 * i + 128] for i in range(4)])
    PK[0] = jnp.concatenate([tile, tile], 0)

    got = [
        net.send(PK.at[0], P1.at[4 * a + b], dev(x=(x + a) % 4, y=(y + b) % 4))
        for a in range(4)
        for b in range(4)
        if a or b
    ]

    def flip(dr):
        return (1 - h if dr // 2 else h), (1 - c if dr % 2 else c)

    sent_e = []
    for dr in (3, 2, 1, 0):
        h2, c2 = flip(dr)
        for d in (2, 1, 3, 0):
            if dr or d:
                to = (y + d) % 4
                sent_e.append(net.send(Pq.at[2 * h2 + c2, to], X.at[dr, y], dev(h=h2, c=c2, y=to)))
    peak = PK[0]
    for cp in got:
        cp.wait_recv()
    for i in range(1, 16):
        peak = jnp.maximum(peak, P1[i])
    PK[1] = peak
    got = []
    for dr in (3, 2, 1, 0):
        h2, c2 = flip(dr)
        for e in (1, 0):
            if dr or e:
                got.append(
                    net.send(PK.at[1], P2.at[e, dr], dev(h=h2, c=c2, z=zp if e else z))
                )
    for cp in sm + sent_e:
        cp.wait_recv()
    for cp in got:
        cp.wait_recv()
    factors = []
    for dr in range(4):
        high = jnp.maximum(P2[0, dr] if dr else peak, P2[1, dr])
        high = jnp.max(high, axis=(0, 1), keepdims=True)
        factors.append(0.5 / jnp.maximum(high, 0.5))
    X[0, y] = Pq[rep, y]
    new = []
    for ys in range(4):
        terms = [X[dr, ys].astype(F32) * factors[dr] for dr in range(4)]
        avg = functools.reduce(jnp.add, terms) / 4
        new.append(SX[ys, 0] - 0.7 * (avg + 0.9 * (0.9 * SX[ys, 1] + avg)))
    for p in range(2):
        for t in range(2):
            Wb[p, :, pl.ds(t * 128, 128)] = jnp.concatenate(
                [rows4(v, 2 * p + t) for v in new], 0
            ).astype(BF16)

    def small(p):
        return w_out.at[z, x, :, pl.ds(mo((2 * h + c) * 2048 + p * 1024 + y * 256), 256)]

    for p in range(2):
        cp = pltpu.make_async_copy(Wb.at[p], small(p), ls.at[p])
        cp.start()
        loc[p] = cp
    strips = [[], []]
    for s in range(2):
        for d in (2, 1, 3, 0):
            if s or d:
                for p in range(2):
                    to = dev(h=1 - h if s else h, z=(z + d) % 4)
                    strips[s].append(net.send(Wb.at[p], small(p), to))

    wide_e = []
    for dr in (3, 2, 1):
        h2, c2 = flip(dr)
        wide_e.append(net.send(Pq.at[2 * h2 + c2], E.at[dr], dev(h=h2, c=c2)))

    def part(p, s, mid, last):
        q = 2 * (1 - h if s else h) + c
        if p == 0:
            return w_out.at[:, last, :, pl.ds(mo(q * 2048 + mid * 256), 256)]
        return w_out.at[:, mid, :, pl.ds(mo(q * 2048 + 1024 + last * 256), 256)]

    def large(p, s, last):
        q = 2 * (1 - h if s else h) + c
        if p == 0:
            return w_out.at[:, last, :, pl.ds(mo(q * 2048), 1024)]
        return w_out.at[:, :, :, pl.ds(mo(q * 2048 + 1024 + last * 256), 256)]

    ways = ((y, x, xn, xp), (x, y, yn, yp))
    mids, near, far, swaps = {}, {}, [], []

    def send_mid(s):
        for d in (2, 1, 3):
            for p, (m, la, _, _) in enumerate(ways):
                to = dev(y=(y + d) % 4) if p == 0 else dev(x=(x + d) % 4)
                mids[p, s, d] = net.send(part(p, s, m, la), part(p, s, m, la), to)

    def send_last(s, d):
        for p, (m, la, nx, pv) in enumerate(ways):
            if d:
                mids[p, s, d].wait_recv()
            blk = part(p, s, (m + 4 - d) % 4, la)
            near[p, s, d] = net.send(blk, blk, nx), net.send(blk, blk, pv)

    def pass_on(s, d):
        for p, (m, la, nx, pv) in enumerate(ways):
            mid = (m + 4 - d) % 4
            from_prev, from_next = near[p, s, d]
            if d % 2 == 0:
                from_prev.wait_recv()
                blk = part(p, s, mid, (la + 3) % 4)
                far.append(net.send(blk, blk, nx))
                from_next.wait_recv()
            else:
                from_next.wait_recv()
                blk = part(p, s, mid, (la + 1) % 4)
                far.append(net.send(blk, blk, pv))
                from_prev.wait_recv()

    def swap(s, d):
        for p, (m, la, nx, pv) in enumerate(ways):
            blk = large(p, s, (la + 4 - d) % 4)
            swaps.append(net.send(blk, blk, sib))

    for p in range(2):
        loc[p].wait()
    for s in range(2):
        for cp in strips[s]:
            cp.wait_recv()
        send_mid(s)
        send_last(s, 0)

    order = (1, 3, 2)
    for d in order:
        send_last(0, d)
    swap(0, 0)
    pass_on(0, 0)
    for d in order:
        send_last(1, d)
    swap(1, 0)
    for cp in wide_e:
        cp.wait_recv()
    for yy in range(4):
        terms = [
            (E[dr, yy] if dr else Pq[rep, yy]).astype(F32) * factors[dr] for dr in range(4)
        ]
        averaged = functools.reduce(jnp.add, terms) / 4
        m_new = 0.9 * SM[yy, 1] + averaged
        p_new = SM[yy, 0] - 0.7 * (averaged + 0.9 * m_new)
        for b, o in enumerate(offsets(yy)):
            mn_out[:, o : o + 128] = rows4(m_new, b)
            pn_out[:, o : o + 128] = rows4(p_new, b)

    for d in order:
        pass_on(0, d)
    swap(0, 1)
    swap(0, 3)
    pass_on(1, 0)
    for d in order:
        pass_on(1, d)
    swap(1, 1)
    swap(1, 3)
    for cp in far[:8]:
        cp.wait_recv()
    swap(0, 2)
    for cp in far[8:]:
        cp.wait_recv()
    swap(1, 2)
    for cp in swaps:
        cp.wait_recv()
    for cp in net.sent:
        cp.wait_send()


def flush(*refs):
    n = len(refs) // 2
    sems = refs[2 * n]
    cps = [pltpu.make_async_copy(refs[i], refs[n + i], sems.at[i]) for i in range(n)]
    for cp in cps:
        cp.start()
    for cp in cps:
        cp.wait()


def local(grad_parts, adam_m, adam_v, params_inner, snapshot, momentum):
    vmem = pl.BlockSpec(memory_space=pltpu.VMEM)
    hbm = pl.BlockSpec(memory_space=pl.ANY)
    V = pltpu.VMEM
    args = (
        grad_parts.reshape(4, 4, 16, D),
        adam_m[0],
        adam_v[0],
        params_inner[0],
        snapshot,
        momentum,
    )
    outs = pl.pallas_call(
        kernel,
        out_shape=(
            jax.ShapeDtypeStruct((4, D), F32),
            jax.ShapeDtypeStruct((4, D), F32),
            jax.ShapeDtypeStruct((4, 2048), F32),
            jax.ShapeDtypeStruct((4, 2048), F32),
            jax.ShapeDtypeStruct((4, 4, 16, D), BF16),
        ),
        in_specs=[pl.BlockSpec(memory_space=pltpu.HBM)] * 6,
        out_specs=(vmem, vmem, vmem, vmem, hbm),
        scratch_shapes=[
            V((4, D), F32),
            V((4, D), F32),
            V((4, D), F32),
            V((4, D), F32),
            V((4, D), F32),
            V((4, 4, 16, D), BF16),
            V((K, 2, 3, 2, 16, W), BF16),
            V((K, 2, 3, 2, 4, 16, CW), BF16),
            V((K, 2, 2, 16, W), BF16),
            V((K, 2, 2, 4, 16, CW), BF16),
            V((K, 4, 16, W), BF16),
            V((K, 4, 4, 16, CW), BF16),
            V((NR, 2, 3, 2, 16, CW), BF16),
            V((NR, 2, 2, 16, CW), BF16),
            V((K, 4, 4, 16, HW), BF16),
            V((K, 4, 4, 16, HW), BF16),
            V((4, D), F32),
            V((2, 8, 128), F32),
            V((16, 8, 128), F32),
            V((2, 4, 8, 128), F32),
            V((4, 4, 16, 128), BF16),
            V((4, 4, 16, 128), BF16),
            V((4, 4, 16, 128), BF16),
            V((4, 2, 16, 128), F32),
            V((4, 2, 16, 128), F32),
            V((2, 16, 256), BF16),
            pltpu.SemaphoreType.DMA((NSEM,)),
            pltpu.SemaphoreType.DMA((NSEM,)),
            pltpu.SemaphoreType.DMA((NR + 5,)),
            pltpu.SemaphoreType.REGULAR((4,)),
        ],
        compiler_params=pltpu.CompilerParams(
            collective_id=0, has_side_effects=True, vmem_limit_bytes=40 * 2**20
        ),
        name="outer_step",
    )(*[pltpu.with_memory_space_constraint(a, pltpu.HBM) for a in args])
    m, v, pn, mn, w = pl.pallas_call(
        flush,
        out_shape=tuple(jax.ShapeDtypeStruct(o.shape, o.dtype) for o in outs),
        in_specs=[hbm] * 5,
        out_specs=(hbm,) * 5,
        scratch_shapes=[pltpu.SemaphoreType.DMA((5,))],
        compiler_params=pltpu.CompilerParams(vmem_limit_bytes=2**20),
        name="write_out",
    )(*outs)
    return m[None], v[None], pn, mn, w.reshape(256, D)


def solution(mesh):
    rows = P("rep", "fsdp", None)
    flat = P("fsdp", None)
    return jax.shard_map(
        local,
        mesh=mesh,
        in_specs=(rows, rows, rows, rows, flat, flat),
        out_specs=(rows, rows, P("fsdp", "rep"), P("fsdp", "rep"), P()),
        check_vma=False,
    )
```

```python
import functools

import jax
import jax.numpy as jnp
from jax import lax
from jax.experimental import pallas as pl
from jax.experimental.pallas import tpu as pltpu
from jax.sharding import PartitionSpec as P

D = 8192
K = 2
PIECE = (256, 128)
NR = 2 * K
WS = (2048, 1536)
CWS = tuple(w // 4 for w in WS)
ZO = 2 * sum(WS)
ZW = D - ZO
NSEM = 260
F32 = jnp.float32
BF16 = jnp.bfloat16


def mo(v, m=128):
    return pl.multiple_of(v, m)


class Ring:
    def __init__(self, net, i, to_next, to_prev, raw, own, land, acc):
        self.net, self.i = net, i
        self.to_next, self.to_prev = to_next, to_prev
        self.raw, self.own, self.land, self.acc = raw, own, land, acc

    def start(self):
        self.start_far()
        self.start_near()

    def start_far(self):
        i, net = self.i, self.net
        far = (i + 2) % 4
        self.a = [
            net.send(self.raw(far, 0), self.land.at[0, 0], self.to_next),
            net.send(self.raw(far, 1), self.land.at[1, 0], self.to_prev),
        ]

    def leave(self, copies):
        for cp in copies:
            cp.wait_send()
            self.net.sent = [other for other in self.net.sent if other is not cp]

    def start_near(self):
        i, net = self.i, self.net
        nxt, prv = (i + 1) % 4, (i + 3) % 4
        self.b = [
            net.send(self.raw(nxt, 1), self.land.at[0, 1], self.to_next),
            net.send(self.raw(prv, 0), self.land.at[1, 1], self.to_prev),
        ]

    def forward(self):
        i, net = self.i, self.net
        nxt, prv = (i + 1) % 4, (i + 3) % 4
        self.a[0].wait_recv()
        add(self.acc.at[0], [self.own(nxt, 0), self.land.at[0, 0]])
        c0 = net.send(self.acc.at[0], self.land.at[0, 2], self.to_next)
        self.a[1].wait_recv()
        add(self.acc.at[1], [self.own(prv, 1), self.land.at[1, 0]])
        c1 = net.send(self.acc.at[1], self.land.at[1, 2], self.to_prev)
        self.c = [c0, c1]

    def wait(self):
        for cp in self.b + self.c:
            cp.wait_recv()

    def terms(self, hh):
        land = self.land
        if hh == 0:
            return [self.own(self.i, 0), land.at[0, 2], land.at[1, 1]]
        return [self.own(self.i, 1), land.at[0, 1], land.at[1, 2]]


class Direct(Ring):
    def __init__(self, net, i, to, raw, land):
        self.net, self.i, self.to, self.own, self.land = net, i, to, raw, land

    def start(self):
        self.b = [
            self.net.send(self.own((self.i + d) % 4, hh), self.land.at[hh, d - 1], self.to[d - 1])
            for d in (2, 1, 3)
            for hh in range(2)
        ]
        self.c = []

    def forward(self):
        pass

    def terms(self, hh):
        return [self.own(self.i, hh)] + [self.land.at[hh, d] for d in range(3)]


def add(dst, srcs):
    shape = dst.shape
    if len(shape) == 4:

        def body(j, _):
            dst[:, j] = functools.reduce(
                jnp.add, [s[:, j].astype(F32) for s in srcs]
            ).astype(BF16)
            return 0

        lax.fori_loop(0, shape[1], body, 0)
    else:

        def body(j, _):
            at = pl.ds(mo(j * step, step), step)
            dst[:, :, at] = functools.reduce(
                jnp.add, [s[:, :, at].astype(F32) for s in srcs]
            ).astype(BF16)
            return 0

        step = 512 if shape[2] % 512 == 0 else shape[2]
        lax.fori_loop(0, shape[2] // step, body, 0)


class Net:
    def __init__(self, ss, rs):
        self.ss, self.rs, self.n = ss, rs, 0
        self.sent = []

    def send(self, src, dst, dev):
        n = self.n
        self.n += 1
        assert n < NSEM
        cp = pltpu.make_async_remote_copy(
            src, dst, self.ss.at[n], self.rs.at[n], device_id=dev
        )
        cp.start()
        self.sent.append(cp)
        return cp


def offsets(yy):
    return [p * 1024 + yy * 256 + t * 128 for p in range(2) for t in range(2)]


def rows4(v, b):
    return v[4 * b : 4 * b + 4]


def kernel(
    grad, m_in, v_in, p_in, snap_in, mom_in,
    m_out, v_out, pn_out, mn_out, w_out,
    m_ref, v_ref, p_ref, snap, mom, G, LX1, LY1, AX1, AY1, SX1, SY1, L2, A2, M3, R3, LC1, SC, LC2, MC, RC, Gs, PK, P1, P2, Pq, E, X, SM, SX, Wb,
    ss, rs, ls, bs,
):
    rep, f = lax.axis_index("rep"), lax.axis_index("fsdp")
    h, c = rep // 2, rep % 2
    z, x, y = f // 16, (f // 4) % 4, f % 4
    zp = z + 1 - 2 * (z % 2)
    Z = 4 * h + z

    def dev(h=h, c=c, z=z, x=x, y=y):
        return (2 * h + c, 16 * z + 4 * x + y)

    loc = []
    for r in range(NR):
        at = pl.ds(r * 2048, 2048)
        cp = pltpu.make_async_copy(grad.at[:, :, :, at], G.at[:, :, :, at], ls.at[r])
        cp.start()
        loc.append(cp)

    held = []
    for n, (src, dst) in enumerate(
        ((m_in, m_ref), (v_in, v_ref), (p_in, p_ref), (snap_in, snap), (mom_in, mom))
    ):
        cp = pltpu.make_async_copy(src, dst, ls.at[NR + n])
        cp.start()
        held.append(cp)

    xn, xp = dev(x=(x + 1) % 4), dev(x=(x + 3) % 4)
    yn, yp = dev(y=(y + 1) % 4), dev(y=(y + 3) % 4)
    sib = dev(c=1 - c)
    Zn, Zp = (Z + 1) % 8, (Z + 7) % 8
    line = [dev(h=Zn // 4, z=Zn % 4), dev(h=Zp // 4, z=Zp % 4), sib]
    bar = pltpu.get_barrier_semaphore()
    for d in [xn, xp, yn, yp] + line:
        pl.semaphore_signal(bar, 1, device_id=d)
    pl.semaphore_wait(bar, 7)

    def ahead(n):
        for d in line:
            pl.semaphore_signal(bs.at[n], 1, device_id=d)
        pl.semaphore_wait(bs.at[n], 3)

    net = Net(ss, rs)

    def origin(k, s):
        return 2 * sum(WS[:k]) + s * WS[k]

    def first(r):
        k = r // 2
        o, w, cw = origin(k, r % 2), WS[k], CWS[k]
        if r % 2 == 0:

            def chunk(src, j, hh):
                return src.at[pl.ds(2 * hh, 2), j, :, pl.ds(o, w)]

            return Ring(
                net, x, xn, xp, functools.partial(chunk, grad), functools.partial(chunk, G),
                LX1[k], AX1[k],
            )

        def chunk(src, j, hh):
            return src.at[pl.ds(2 * hh, 2), :, :, pl.ds(mo(o + j * cw), cw)]

        return Ring(
            net, y, yn, yp, functools.partial(chunk, grad), functools.partial(chunk, G),
            LY1[k], AY1[k],
        )

    def second(r):
        k = r // 2
        if r % 2 == 0:

            def chunk(j, hh):
                return SX1[k].at[pl.ds(2 * hh, 2), :, pl.ds(mo(j * CWS[k]), CWS[k])]

            if k == K - 1:
                to = [dev(y=(y + d) % 4) for d in (1, 2, 3)]
                return Direct(net, y, to, chunk, L2[k].at[r % 2])
            return Ring(net, y, yn, yp, chunk, chunk, L2[k].at[r % 2], A2[k].at[r % 2])

        def chunk(j, hh):
            return SY1[k].at[pl.ds(2 * hh, 2), j]

        if k == K - 1:
            to = [dev(x=(x + d) % 4) for d in (1, 2, 3)]
            return Direct(net, x, to, chunk, L2[k].at[r % 2])
        return Ring(net, x, xn, xp, chunk, chunk, L2[k].at[r % 2], A2[k].at[r % 2])

    one = [first(r) for r in range(NR)]
    two = [second(r) for r in range(NR)]

    def finish_first(k):
        for r in (2 * k, 2 * k + 1):
            one[r].wait()
            dst = (SX1 if r % 2 == 0 else SY1)[k]
            for hh in range(2):
                add(dst.at[pl.ds(2 * hh, 2)], one[r].terms(hh))
        for r in (2 * k, 2 * k + 1):
            two[r].start()

    def finish_second(k):
        rings = two[2 * k], two[2 * k + 1]
        for ring in rings:
            ring.wait()
        for zz in range(4):
            pieces = []
            for ring in rings:
                s = functools.reduce(
                    jnp.add, [t[zz % 2].astype(F32) for t in ring.terms(zz // 2)]
                )
                pw = PIECE[k]
                pieces += [s[:, o : o + pw] for o in range(0, CWS[k], pw)]
            while len(pieces) % 4:
                pieces.append(jnp.zeros_like(pieces[0]))
            for yy in range(4):
                M3[k][zz, yy] = jnp.concatenate([rows4(s, yy) for s in pieces], 0).astype(BF16)
        return [
            net.send(
                M3[k].at[(z + dz) % 4, (y + dy) % 4],
                R3[k].at[dz, dy],
                dev(z=(z + dz) % 4, y=(y + dy) % 4),
            )
            for dz in (2, 1, 3, 0)
            for dy in range(4)
            if dz or dy
        ]

    one[0].start_far()
    one[1].start_far()
    ahead(0)
    ahead(1)
    one[0].leave(one[0].a + one[1].a)
    one[0].start_near()
    one[1].start_near()
    one[2].start_far()
    one[3].start_far()
    ahead(2)
    ahead(3)
    zcols = pl.ds(ZO, ZW)
    zfirst = [
        net.send(grad.at[(z + d) % 4, :, :, zcols], LC1.at[d - 1], dev(z=(z + d) % 4))
        for d in (2, 1, 3)
    ]
    for cp in loc:
        cp.wait()
    one[0].forward()
    one[1].forward()
    one[0].leave(one[0].c + one[1].c)
    one[2].start_near()
    one[3].start_near()
    finish_first(0)
    one[2].forward()
    one[3].forward()
    two[0].forward()
    two[1].forward()
    finish_first(1)
    for cp in zfirst:
        cp.wait_recv()
    add(SC, [G.at[z, :, :, zcols]] + [LC1.at[d] for d in range(3)])
    zsecond = [
        net.send(SC.at[(x + d) % 4], LC2.at[d - 1], dev(x=(x + d) % 4)) for d in (2, 1, 3)
    ]
    third = finish_second(0)
    for cp in held:
        cp.wait()
    for n, ref in enumerate((snap, mom)):
        for yy in range(4):
            SM[yy, n] = jnp.concatenate(
                [ref[:, pl.ds(mo(rep * 2048 + o), 128)] for o in offsets(yy)], 0
            )
    sm = [net.send(SM.at[(y + d) % 4], SX.at[y], dev(y=(y + d) % 4)) for d in (2, 1, 3)]
    SX[y] = SM[y]
    two[2].forward()
    two[3].forward()
    third += finish_second(1)
    for cp in zsecond:
        cp.wait_recv()
    s = SC[x].astype(F32)
    for d in range(3):
        s = s + LC2[d].astype(F32)
    for yy in range(4):
        MC[yy] = jnp.concatenate(
            [rows4(s[:, t * ZW // 4 : (t + 1) * ZW // 4], yy) for t in range(4)], 0
        ).astype(BF16)
    third += [
        net.send(MC.at[(y + d) % 4], RC.at[d - 1], dev(y=(y + d) % 4)) for d in (2, 1, 3)
    ]
    for cp in third:
        cp.wait_recv()
    for k in range(K):
        for dy in range(4):
            g = None
            for dz in range(4):
                t = (R3[k][dz, dy] if dz or dy else M3[k][z, y]).astype(F32)
                g = t if g is None else g + t
            ys = (y + 4 - dy) % 4
            pw = PIECE[k]
            n = CWS[k] // pw
            for s in range(2):
                for t in range(n):
                    at = pl.ds(mo(origin(k, s) + ys * CWS[k] + t * pw), pw)
                    Gs[:, at] = rows4(g, n * s + t)
    g = MC[y].astype(F32)
    for d in range(3):
        g = g + RC[d].astype(F32)
    for t in range(4):
        Gs[:, ZO + t * ZW // 4 : ZO + (t + 1) * ZW // 4] = rows4(g, t)

    top = None
    for q in range(4):
        parts = []
        for t in range(4):
            at = pl.ds(q * 2048 + t * 512, 512)
            g, params = Gs[:, at], p_ref[:, at]
            m_next = 0.9 * m_ref[:, at] + 0.1 * g
            v_next = 0.95 * v_ref[:, at] + 0.05 * g * g
            m_out[:, at] = m_next
            v_out[:, at] = v_next
            inner = params - 0.02 * (m_next / (jnp.sqrt(v_next) + 1e-8) + 0.1 * params)
            pseudo = snap[:, at] - inner
            parts.append(pseudo)
            size = jnp.abs(pseudo)
            top = size if top is None else jnp.maximum(top, size)
        wide = jnp.concatenate(parts, 1)
        for yy in range(4):
            Pq[q, yy] = jnp.concatenate([wide[:, o : o + 128] for o in offsets(yy)], 0).astype(BF16)
    tile = functools.reduce(jnp.maximum, [top[:, 128 * i : 128 * i + 128] for i in range(4)])
    PK[0] = jnp.concatenate([tile, tile], 0)

    got = [
        net.send(PK.at[0], P1.at[4 * a + b], dev(x=(x + a) % 4, y=(y + b) % 4))
        for a in range(4)
        for b in range(4)
        if a or b
    ]

    def flip(dr):
        return (1 - h if dr // 2 else h), (1 - c if dr % 2 else c)

    sent_e = []
    for dr in (3, 2, 1, 0):
        h2, c2 = flip(dr)
        for d in (2, 1, 3, 0):
            if dr or d:
                to = (y + d) % 4
                sent_e.append(net.send(Pq.at[2 * h2 + c2, to], X.at[dr, y], dev(h=h2, c=c2, y=to)))
    peak = PK[0]
    for cp in got:
        cp.wait_recv()
    for i in range(1, 16):
        peak = jnp.maximum(peak, P1[i])
    PK[1] = peak
    got = []
    for dr in (3, 2, 1, 0):
        h2, c2 = flip(dr)
        for e in (1, 0):
            if dr or e:
                got.append(
                    net.send(PK.at[1], P2.at[e, dr], dev(h=h2, c=c2, z=zp if e else z))
                )
    for cp in sm + sent_e:
        cp.wait_recv()
    for cp in got:
        cp.wait_recv()
    factors = []
    for dr in range(4):
        high = jnp.maximum(P2[0, dr] if dr else peak, P2[1, dr])
        high = jnp.max(high, axis=(0, 1), keepdims=True)
        factors.append(0.5 / jnp.maximum(high, 0.5))
    X[0, y] = Pq[rep, y]
    new = []
    for ys in range(4):
        terms = [X[dr, ys].astype(F32) * factors[dr] for dr in range(4)]
        avg = functools.reduce(jnp.add, terms) / 4
        new.append(SX[ys, 0] - 0.7 * (avg + 0.9 * (0.9 * SX[ys, 1] + avg)))
    for p in range(2):
        for t in range(2):
            Wb[p, :, pl.ds(t * 128, 128)] = jnp.concatenate(
                [rows4(v, 2 * p + t) for v in new], 0
            ).astype(BF16)

    def small(p):
        return w_out.at[z, x, :, pl.ds(mo((2 * h + c) * 2048 + p * 1024 + y * 256), 256)]

    for p in range(2):
        cp = pltpu.make_async_copy(Wb.at[p], small(p), ls.at[p])
        cp.start()
        loc[p] = cp
    strips = [[], []]
    for s in range(2):
        for d in (2, 1, 3, 0):
            if s or d:
                for p in range(2):
                    to = dev(h=1 - h if s else h, z=(z + d) % 4)
                    strips[s].append(net.send(Wb.at[p], small(p), to))

    wide_e = []
    for dr in (3, 2, 1):
        h2, c2 = flip(dr)
        wide_e.append(net.send(Pq.at[2 * h2 + c2], E.at[dr], dev(h=h2, c=c2)))

    def part(p, s, mid, last):
        q = 2 * (1 - h if s else h) + c
        if p == 0:
            return w_out.at[:, last, :, pl.ds(mo(q * 2048 + mid * 256), 256)]
        return w_out.at[:, mid, :, pl.ds(mo(q * 2048 + 1024 + last * 256), 256)]

    def large(p, s, last):
        q = 2 * (1 - h if s else h) + c
        if p == 0:
            return w_out.at[:, last, :, pl.ds(mo(q * 2048), 1024)]
        return w_out.at[:, :, :, pl.ds(mo(q * 2048 + 1024 + last * 256), 256)]

    ways = ((y, x, xn, xp), (x, y, yn, yp))
    mids, near, far, swaps = {}, {}, [], []

    def send_mid(s):
        for d in (2, 1, 3):
            for p, (m, la, _, _) in enumerate(ways):
                to = dev(y=(y + d) % 4) if p == 0 else dev(x=(x + d) % 4)
                mids[p, s, d] = net.send(part(p, s, m, la), part(p, s, m, la), to)

    def send_last(s, d):
        for p, (m, la, nx, pv) in enumerate(ways):
            if d:
                mids[p, s, d].wait_recv()
            blk = part(p, s, (m + 4 - d) % 4, la)
            near[p, s, d] = net.send(blk, blk, nx), net.send(blk, blk, pv)

    def pass_on(s, d):
        for p, (m, la, nx, pv) in enumerate(ways):
            mid = (m + 4 - d) % 4
            from_prev, from_next = near[p, s, d]
            if d % 2 == 0:
                from_prev.wait_recv()
                blk = part(p, s, mid, (la + 3) % 4)
                far.append(net.send(blk, blk, nx))
                from_next.wait_recv()
            else:
                from_next.wait_recv()
                blk = part(p, s, mid, (la + 1) % 4)
                far.append(net.send(blk, blk, pv))
                from_prev.wait_recv()

    def swap(s, d):
        for p, (m, la, nx, pv) in enumerate(ways):
            blk = large(p, s, (la + 4 - d) % 4)
            swaps.append(net.send(blk, blk, sib))

    for p in range(2):
        loc[p].wait()
    for s in range(2):
        for cp in strips[s]:
            cp.wait_recv()
        send_mid(s)
        send_last(s, 0)

    order = (1, 3, 2)
    for d in order:
        send_last(0, d)
    swap(0, 0)
    pass_on(0, 0)
    for d in order:
        send_last(1, d)
    swap(1, 0)
    for cp in wide_e:
        cp.wait_recv()
    for yy in range(4):
        terms = [
            (E[dr, yy] if dr else Pq[rep, yy]).astype(F32) * factors[dr] for dr in range(4)
        ]
        averaged = functools.reduce(jnp.add, terms) / 4
        m_new = 0.9 * SM[yy, 1] + averaged
        p_new = SM[yy, 0] - 0.7 * (averaged + 0.9 * m_new)
        for b, o in enumerate(offsets(yy)):
            mn_out[:, o : o + 128] = rows4(m_new, b)
            pn_out[:, o : o + 128] = rows4(p_new, b)

    for d in order:
        pass_on(0, d)
    swap(0, 1)
    swap(0, 3)
    pass_on(1, 0)
    for d in order:
        pass_on(1, d)
    swap(1, 1)
    swap(1, 3)
    for cp in far[:8]:
        cp.wait_recv()
    swap(0, 2)
    for cp in far[8:]:
        cp.wait_recv()
    swap(1, 2)
    for cp in swaps:
        cp.wait_recv()
    for cp in net.sent:
        cp.wait_send()


def flush(*refs):
    n = len(refs) // 2
    sems = refs[2 * n]
    cps = [pltpu.make_async_copy(refs[i], refs[n + i], sems.at[i]) for i in range(n)]
    for cp in cps:
        cp.start()
    for cp in cps:
        cp.wait()


def local(grad_parts, adam_m, adam_v, params_inner, snapshot, momentum):
    vmem = pl.BlockSpec(memory_space=pltpu.VMEM)
    hbm = pl.BlockSpec(memory_space=pl.ANY)
    V = pltpu.VMEM
    args = (
        grad_parts.reshape(4, 4, 16, D),
        adam_m[0],
        adam_v[0],
        params_inner[0],
        snapshot,
        momentum,
    )
    outs = pl.pallas_call(
        kernel,
        out_shape=(
            jax.ShapeDtypeStruct((4, D), F32),
            jax.ShapeDtypeStruct((4, D), F32),
            jax.ShapeDtypeStruct((4, 2048), F32),
            jax.ShapeDtypeStruct((4, 2048), F32),
            jax.ShapeDtypeStruct((4, 4, 16, D), BF16),
        ),
        in_specs=[pl.BlockSpec(memory_space=pltpu.HBM)] * 6,
        out_specs=(vmem, vmem, vmem, vmem, hbm),
        scratch_shapes=[
            V((4, D), F32),
            V((4, D), F32),
            V((4, D), F32),
            V((4, D), F32),
            V((4, D), F32),
            V((4, 4, 16, D), BF16),
            [V((2, 3, 2, 16, w), BF16) for w in WS],
            [V((2, 3, 2, 4, 16, w), BF16) for w in CWS],
            [V((2, 2, 16, w), BF16) for w in WS],
            [V((2, 2, 4, 16, w), BF16) for w in CWS],
            [V((4, 16, w), BF16) for w in WS],
            [V((4, 4, 16, w), BF16) for w in CWS],
            [V((2, 2, 3, 2, 16, w), BF16) for w in CWS],
            [V((2, 2, 2, 16, w), BF16) for w in CWS],
            [V((4, 4, 16, 256), BF16), V((4, 4, 32, 128), BF16)],
            [V((4, 4, 16, 256), BF16), V((4, 4, 32, 128), BF16)],
            V((3, 4, 16, ZW), BF16),
            V((4, 16, ZW), BF16),
            V((3, 16, ZW), BF16),
            V((4, 16, ZW // 4), BF16),
            V((3, 16, ZW // 4), BF16),
            V((4, D), F32),
            V((2, 8, 128), F32),
            V((16, 8, 128), F32),
            V((2, 4, 8, 128), F32),
            V((4, 4, 16, 128), BF16),
            V((4, 4, 16, 128), BF16),
            V((4, 4, 16, 128), BF16),
            V((4, 2, 16, 128), F32),
            V((4, 2, 16, 128), F32),
            V((2, 16, 256), BF16),
            pltpu.SemaphoreType.DMA((NSEM,)),
            pltpu.SemaphoreType.DMA((NSEM,)),
            pltpu.SemaphoreType.DMA((NR + 5,)),
            pltpu.SemaphoreType.REGULAR((4,)),
        ],
        compiler_params=pltpu.CompilerParams(
            collective_id=0, has_side_effects=True, vmem_limit_bytes=40 * 2**20
        ),
        name="outer_step",
    )(*[pltpu.with_memory_space_constraint(a, pltpu.HBM) for a in args])
    m, v, pn, mn, w = pl.pallas_call(
        flush,
        out_shape=tuple(jax.ShapeDtypeStruct(o.shape, o.dtype) for o in outs),
        in_specs=[hbm] * 5,
        out_specs=(hbm,) * 5,
        scratch_shapes=[pltpu.SemaphoreType.DMA((5,))],
        compiler_params=pltpu.CompilerParams(vmem_limit_bytes=2**20),
        name="write_out",
    )(*outs)
    return m[None], v[None], pn, mn, w.reshape(256, D)


def solution(mesh):
    rows = P("rep", "fsdp", None)
    flat = P("fsdp", None)
    return jax.shard_map(
        local,
        mesh=mesh,
        in_specs=(rows, rows, rows, rows, flat, flat),
        out_specs=(rows, rows, P("fsdp", "rep"), P("fsdp", "rep"), P()),
        check_vma=False,
    )
```

```python
import functools

import jax
import jax.numpy as jnp
from jax import lax
from jax.experimental import pallas as pl
from jax.experimental.pallas import tpu as pltpu
from jax.sharding import PartitionSpec as P

D = 8192
K = 2
PIECE = (256, 128)
NR = 2 * K
WS = (2048, 1536)
CWS = tuple(w // 4 for w in WS)
ZO = 2 * sum(WS)
ZW = D - ZO
NSEM = 260
F32 = jnp.float32
BF16 = jnp.bfloat16


def mo(v, m=128):
    return pl.multiple_of(v, m)


class Ring:
    def __init__(self, net, i, to_next, to_prev, raw, own, land, acc):
        self.net, self.i = net, i
        self.to_next, self.to_prev = to_next, to_prev
        self.raw, self.own, self.land, self.acc = raw, own, land, acc

    def start(self):
        self.start_far()
        self.start_near()

    def start_far(self):
        i, net = self.i, self.net
        far = (i + 2) % 4
        self.a = [
            net.send(self.raw(far, 0), self.land.at[0, 0], self.to_next),
            net.send(self.raw(far, 1), self.land.at[1, 0], self.to_prev),
        ]

    def leave(self, copies):
        for cp in copies:
            cp.wait_send()
            self.net.sent = [other for other in self.net.sent if other is not cp]

    def start_near(self):
        i, net = self.i, self.net
        nxt, prv = (i + 1) % 4, (i + 3) % 4
        self.b = [
            net.send(self.raw(nxt, 1), self.land.at[0, 1], self.to_next),
            net.send(self.raw(prv, 0), self.land.at[1, 1], self.to_prev),
        ]

    def forward(self):
        i, net = self.i, self.net
        nxt, prv = (i + 1) % 4, (i + 3) % 4
        self.a[0].wait_recv()
        add(self.acc.at[0], [self.own(nxt, 0), self.land.at[0, 0]])
        c0 = net.send(self.acc.at[0], self.land.at[0, 2], self.to_next)
        self.a[1].wait_recv()
        add(self.acc.at[1], [self.own(prv, 1), self.land.at[1, 0]])
        c1 = net.send(self.acc.at[1], self.land.at[1, 2], self.to_prev)
        self.c = [c0, c1]

    def wait(self):
        for cp in self.b + self.c:
            cp.wait_recv()

    def terms(self, hh):
        land = self.land
        if hh == 0:
            return [self.own(self.i, 0), land.at[0, 2], land.at[1, 1]]
        return [self.own(self.i, 1), land.at[0, 1], land.at[1, 2]]


class Direct(Ring):
    def __init__(self, net, i, to, raw, land):
        self.net, self.i, self.to, self.own, self.land = net, i, to, raw, land

    def start(self):
        self.b = [
            self.net.send(self.own((self.i + d) % 4, hh), self.land.at[hh, d - 1], self.to[d - 1])
            for d in (2, 1, 3)
            for hh in range(2)
        ]
        self.c = []

    def forward(self):
        pass

    def terms(self, hh):
        return [self.own(self.i, hh)] + [self.land.at[hh, d] for d in range(3)]


def add(dst, srcs):
    shape = dst.shape
    if len(shape) == 4:

        def body(j, _):
            dst[:, j] = functools.reduce(
                jnp.add, [s[:, j].astype(F32) for s in srcs]
            ).astype(BF16)
            return 0

        lax.fori_loop(0, shape[1], body, 0)
    else:

        def body(j, _):
            at = pl.ds(mo(j * step, step), step)
            dst[:, :, at] = functools.reduce(
                jnp.add, [s[:, :, at].astype(F32) for s in srcs]
            ).astype(BF16)
            return 0

        step = 512 if shape[2] % 512 == 0 else shape[2]
        lax.fori_loop(0, shape[2] // step, body, 0)


class Net:
    def __init__(self, ss, rs):
        self.ss, self.rs, self.n = ss, rs, 0
        self.sent = []

    def send(self, src, dst, dev):
        n = self.n
        self.n += 1
        assert n < NSEM
        cp = pltpu.make_async_remote_copy(
            src, dst, self.ss.at[n], self.rs.at[n], device_id=dev
        )
        cp.start()
        self.sent.append(cp)
        return cp


def offsets(yy):
    return [p * 1024 + yy * 256 + t * 128 for p in range(2) for t in range(2)]


def rows4(v, b):
    return v[4 * b : 4 * b + 4]


def kernel(
    grad, m_in, v_in, p_in, snap_in, mom_in,
    m_out, v_out, pn_out, mn_out, w_out,
    m_ref, v_ref, p_ref, snap, mom, G, LX1, LY1, AX1, AY1, SX1, SY1, L2, A2, M3, R3, LC1, SC, LC2, MC, RC, Gs, PK, P1, P2, Pq, E, X, SM, SX, Wb,
    ss, rs, ls, bs,
):
    rep, f = lax.axis_index("rep"), lax.axis_index("fsdp")
    h, c = rep // 2, rep % 2
    z, x, y = f // 16, (f // 4) % 4, f % 4
    zp = z + 1 - 2 * (z % 2)
    Z = 4 * h + z

    def dev(h=h, c=c, z=z, x=x, y=y):
        return (2 * h + c, 16 * z + 4 * x + y)

    loc = []
    for r in range(NR):
        at = pl.ds(r * 2048, 2048)
        cp = pltpu.make_async_copy(grad.at[:, :, :, at], G.at[:, :, :, at], ls.at[r])
        cp.start()
        loc.append(cp)

    held = []
    for n, (src, dst) in enumerate(
        ((m_in, m_ref), (v_in, v_ref), (p_in, p_ref), (snap_in, snap), (mom_in, mom))
    ):
        cp = pltpu.make_async_copy(src, dst, ls.at[NR + n])
        cp.start()
        held.append(cp)

    xn, xp = dev(x=(x + 1) % 4), dev(x=(x + 3) % 4)
    yn, yp = dev(y=(y + 1) % 4), dev(y=(y + 3) % 4)
    sib = dev(c=1 - c)
    Zn, Zp = (Z + 1) % 8, (Z + 7) % 8
    line = [dev(h=Zn // 4, z=Zn % 4), dev(h=Zp // 4, z=Zp % 4), sib]
    bar = pltpu.get_barrier_semaphore()
    for d in [xn, xp, yn, yp] + line:
        pl.semaphore_signal(bar, 1, device_id=d)
    pl.semaphore_wait(bar, 7)

    def ahead(n):
        for d in line:
            pl.semaphore_signal(bs.at[n], 1, device_id=d)
        pl.semaphore_wait(bs.at[n], 3)

    net = Net(ss, rs)

    def origin(k, s):
        return 2 * sum(WS[:k]) + s * WS[k]

    def first(r):
        k = r // 2
        o, w, cw = origin(k, r % 2), WS[k], CWS[k]
        if r % 2 == 0:

            def chunk(src, j, hh):
                return src.at[pl.ds(2 * hh, 2), j, :, pl.ds(o, w)]

            return Ring(
                net, x, xn, xp, functools.partial(chunk, grad), functools.partial(chunk, G),
                LX1[k], AX1[k],
            )

        def chunk(src, j, hh):
            return src.at[pl.ds(2 * hh, 2), :, :, pl.ds(mo(o + j * cw), cw)]

        return Ring(
            net, y, yn, yp, functools.partial(chunk, grad), functools.partial(chunk, G),
            LY1[k], AY1[k],
        )

    def second(r):
        k = r // 2
        if r % 2 == 0:

            def chunk(j, hh):
                return SX1[k].at[pl.ds(2 * hh, 2), :, pl.ds(mo(j * CWS[k]), CWS[k])]

            if k == K - 1:
                to = [dev(y=(y + d) % 4) for d in (1, 2, 3)]
                return Direct(net, y, to, chunk, L2[k].at[r % 2])
            return Ring(net, y, yn, yp, chunk, chunk, L2[k].at[r % 2], A2[k].at[r % 2])

        def chunk(j, hh):
            return SY1[k].at[pl.ds(2 * hh, 2), j]

        if k == K - 1:
            to = [dev(x=(x + d) % 4) for d in (1, 2, 3)]
            return Direct(net, x, to, chunk, L2[k].at[r % 2])
        return Ring(net, x, xn, xp, chunk, chunk, L2[k].at[r % 2], A2[k].at[r % 2])

    one = [first(r) for r in range(NR)]
    two = [second(r) for r in range(NR)]

    def finish_first(k):
        for r in (2 * k, 2 * k + 1):
            one[r].wait()
            dst = (SX1 if r % 2 == 0 else SY1)[k]
            for hh in range(2):
                add(dst.at[pl.ds(2 * hh, 2)], one[r].terms(hh))
        for r in (2 * k, 2 * k + 1):
            two[r].start()

    def finish_second(k):
        rings = two[2 * k], two[2 * k + 1]
        for ring in rings:
            ring.wait()
        for zz in range(4):
            pieces = []
            for ring in rings:
                s = functools.reduce(
                    jnp.add, [t[zz % 2].astype(F32) for t in ring.terms(zz // 2)]
                )
                pw = PIECE[k]
                pieces += [s[:, o : o + pw] for o in range(0, CWS[k], pw)]
            while len(pieces) % 4:
                pieces.append(jnp.zeros_like(pieces[0]))
            for yy in range(4):
                M3[k][zz, yy] = jnp.concatenate([rows4(s, yy) for s in pieces], 0).astype(BF16)
        return [
            net.send(
                M3[k].at[(z + dz) % 4, (y + dy) % 4],
                R3[k].at[dz, dy],
                dev(z=(z + dz) % 4, y=(y + dy) % 4),
            )
            for dz in (2, 1, 3, 0)
            for dy in range(4)
            if dz or dy
        ]

    one[0].start_far()
    one[1].start_far()
    ahead(0)
    ahead(1)
    one[0].leave(one[0].a + one[1].a)
    one[0].start_near()
    one[1].start_near()
    one[2].start_far()
    one[3].start_far()
    ahead(2)
    ahead(3)
    zcols = pl.ds(ZO, ZW)
    zfirst = [
        net.send(grad.at[(z + d) % 4, :, :, zcols], LC1.at[d - 1], dev(z=(z + d) % 4))
        for d in (2, 1, 3)
    ]
    for cp in loc:
        cp.wait()
    one[0].forward()
    one[1].forward()
    one[0].leave(one[0].c + one[1].c)
    one[2].start_near()
    one[3].start_near()
    finish_first(0)
    one[2].forward()
    one[3].forward()
    two[0].forward()
    two[1].forward()
    finish_first(1)
    for cp in zfirst:
        cp.wait_recv()
    add(SC, [G.at[z, :, :, zcols]] + [LC1.at[d] for d in range(3)])
    zsecond = [
        net.send(SC.at[(x + d) % 4], LC2.at[d - 1], dev(x=(x + d) % 4)) for d in (2, 1, 3)
    ]
    early = finish_second(0)
    for cp in held:
        cp.wait()
    for n, ref in enumerate((snap, mom)):
        for yy in range(4):
            SM[yy, n] = jnp.concatenate(
                [ref[:, pl.ds(mo(rep * 2048 + o), 128)] for o in offsets(yy)], 0
            )
    sm = [net.send(SM.at[(y + d) % 4], SX.at[y], dev(y=(y + d) % 4)) for d in (2, 1, 3)]
    SX[y] = SM[y]
    two[2].forward()
    two[3].forward()
    third = finish_second(1)
    for cp in zsecond:
        cp.wait_recv()
    s = SC[x].astype(F32)
    for d in range(3):
        s = s + LC2[d].astype(F32)
    for yy in range(4):
        MC[yy] = jnp.concatenate(
            [rows4(s[:, t * ZW // 4 : (t + 1) * ZW // 4], yy) for t in range(4)], 0
        ).astype(BF16)
    third += [
        net.send(MC.at[(y + d) % 4], RC.at[d - 1], dev(y=(y + d) % 4)) for d in (2, 1, 3)
    ]

    def collect(k):
        for dy in range(4):
            g = None
            for dz in range(4):
                t = (R3[k][dz, dy] if dz or dy else M3[k][z, y]).astype(F32)
                g = t if g is None else g + t
            ys = (y + 4 - dy) % 4
            pw = PIECE[k]
            n = CWS[k] // pw
            for s in range(2):
                for t in range(n):
                    at = pl.ds(mo(origin(k, s) + ys * CWS[k] + t * pw), pw)
                    Gs[:, at] = rows4(g, n * s + t)
    def adam(q, top):
        parts = []
        for t in range(4):
            at = pl.ds(q * 2048 + t * 512, 512)
            g, params = Gs[:, at], p_ref[:, at]
            m_next = 0.9 * m_ref[:, at] + 0.1 * g
            v_next = 0.95 * v_ref[:, at] + 0.05 * g * g
            m_out[:, at] = m_next
            v_out[:, at] = v_next
            inner = params - 0.02 * (m_next / (jnp.sqrt(v_next) + 1e-8) + 0.1 * params)
            pseudo = snap[:, at] - inner
            parts.append(pseudo)
            size = jnp.abs(pseudo)
            top = size if top is None else jnp.maximum(top, size)
        wide = jnp.concatenate(parts, 1)
        for yy in range(4):
            Pq[q, yy] = jnp.concatenate([wide[:, o : o + 128] for o in offsets(yy)], 0).astype(BF16)
        return top

    for cp in early:
        cp.wait_recv()
    collect(0)
    top = adam(1, adam(0, None))
    for cp in third:
        cp.wait_recv()
    collect(1)
    g = MC[y].astype(F32)
    for d in range(3):
        g = g + RC[d].astype(F32)
    for t in range(4):
        Gs[:, ZO + t * ZW // 4 : ZO + (t + 1) * ZW // 4] = rows4(g, t)
    top = adam(3, adam(2, top))
    tile = functools.reduce(jnp.maximum, [top[:, 128 * i : 128 * i + 128] for i in range(4)])
    PK[0] = jnp.concatenate([tile, tile], 0)

    got = [
        net.send(PK.at[0], P1.at[4 * a + b], dev(x=(x + a) % 4, y=(y + b) % 4))
        for a in (2, 1, 3, 0)
        for b in (2, 1, 3, 0)
        if a or b
    ]

    def flip(dr):
        return (1 - h if dr // 2 else h), (1 - c if dr % 2 else c)

    sent_e = []
    for dr in (3, 2, 1, 0):
        h2, c2 = flip(dr)
        for d in (2, 1, 3, 0):
            if dr or d:
                to = (y + d) % 4
                sent_e.append(net.send(Pq.at[2 * h2 + c2, to], X.at[dr, y], dev(h=h2, c=c2, y=to)))
    peak = PK[0]
    for cp in got:
        cp.wait_recv()
    for i in range(1, 16):
        peak = jnp.maximum(peak, P1[i])
    PK[1] = peak
    got = []
    for dr in (3, 2, 1, 0):
        h2, c2 = flip(dr)
        for e in (1, 0):
            if dr or e:
                got.append(
                    net.send(PK.at[1], P2.at[e, dr], dev(h=h2, c=c2, z=zp if e else z))
                )
    for cp in sm + sent_e:
        cp.wait_recv()
    for cp in got:
        cp.wait_recv()
    factors = []
    for dr in range(4):
        high = jnp.maximum(P2[0, dr] if dr else peak, P2[1, dr])
        high = jnp.max(high, axis=(0, 1), keepdims=True)
        factors.append(0.5 / jnp.maximum(high, 0.5))
    X[0, y] = Pq[rep, y]
    new = []
    for ys in range(4):
        terms = [X[dr, ys].astype(F32) * factors[dr] for dr in range(4)]
        avg = functools.reduce(jnp.add, terms) / 4
        new.append(SX[ys, 0] - 0.7 * (avg + 0.9 * (0.9 * SX[ys, 1] + avg)))
    for p in range(2):
        for t in range(2):
            Wb[p, :, pl.ds(t * 128, 128)] = jnp.concatenate(
                [rows4(v, 2 * p + t) for v in new], 0
            ).astype(BF16)

    def small(p):
        return w_out.at[z, x, :, pl.ds(mo((2 * h + c) * 2048 + p * 1024 + y * 256), 256)]

    for p in range(2):
        cp = pltpu.make_async_copy(Wb.at[p], small(p), ls.at[p])
        cp.start()
        loc[p] = cp
    strips = [[], []]
    for s in range(2):
        for d in (2, 1, 3, 0):
            if s or d:
                for p in range(2):
                    to = dev(h=1 - h if s else h, z=(z + d) % 4)
                    strips[s].append(net.send(Wb.at[p], small(p), to))

    wide_e = []
    for dr in (3, 2, 1):
        h2, c2 = flip(dr)
        wide_e.append(net.send(Pq.at[2 * h2 + c2], E.at[dr], dev(h=h2, c=c2)))

    def part(p, s, mid, last):
        q = 2 * (1 - h if s else h) + c
        if p == 0:
            return w_out.at[:, last, :, pl.ds(mo(q * 2048 + mid * 256), 256)]
        return w_out.at[:, mid, :, pl.ds(mo(q * 2048 + 1024 + last * 256), 256)]

    def large(p, s, last):
        q = 2 * (1 - h if s else h) + c
        if p == 0:
            return w_out.at[:, last, :, pl.ds(mo(q * 2048), 1024)]
        return w_out.at[:, :, :, pl.ds(mo(q * 2048 + 1024 + last * 256), 256)]

    ways = ((y, x, xn, xp), (x, y, yn, yp))
    mids, near, far, swaps = {}, {}, [], []

    def send_mid(s):
        for d in (2, 1, 3):
            for p, (m, la, _, _) in enumerate(ways):
                to = dev(y=(y + d) % 4) if p == 0 else dev(x=(x + d) % 4)
                mids[p, s, d] = net.send(part(p, s, m, la), part(p, s, m, la), to)

    def send_last(s, d):
        for p, (m, la, nx, pv) in enumerate(ways):
            if d:
                mids[p, s, d].wait_recv()
            blk = part(p, s, (m + 4 - d) % 4, la)
            near[p, s, d] = net.send(blk, blk, nx), net.send(blk, blk, pv)

    def pass_on(s, d):
        for p, (m, la, nx, pv) in enumerate(ways):
            mid = (m + 4 - d) % 4
            from_prev, from_next = near[p, s, d]
            if d % 2 == 0:
                from_prev.wait_recv()
                blk = part(p, s, mid, (la + 3) % 4)
                far.append(net.send(blk, blk, nx))
                from_next.wait_recv()
            else:
                from_next.wait_recv()
                blk = part(p, s, mid, (la + 1) % 4)
                far.append(net.send(blk, blk, pv))
                from_prev.wait_recv()

    def swap(s, d):
        for p, (m, la, nx, pv) in enumerate(ways):
            blk = large(p, s, (la + 4 - d) % 4)
            swaps.append(net.send(blk, blk, sib))

    for p in range(2):
        loc[p].wait()
    for s in range(2):
        for cp in strips[s]:
            cp.wait_recv()
        send_mid(s)
        send_last(s, 0)

    order = (1, 3, 2)
    for d in order:
        send_last(0, d)
    swap(0, 0)
    pass_on(0, 0)
    for d in order:
        send_last(1, d)
    swap(1, 0)
    for cp in wide_e:
        cp.wait_recv()
    for yy in range(4):
        terms = [
            (E[dr, yy] if dr else Pq[rep, yy]).astype(F32) * factors[dr] for dr in range(4)
        ]
        averaged = functools.reduce(jnp.add, terms) / 4
        m_new = 0.9 * SM[yy, 1] + averaged
        p_new = SM[yy, 0] - 0.7 * (averaged + 0.9 * m_new)
        for b, o in enumerate(offsets(yy)):
            mn_out[:, o : o + 128] = rows4(m_new, b)
            pn_out[:, o : o + 128] = rows4(p_new, b)

    for d in order:
        pass_on(0, d)
    swap(0, 1)
    swap(0, 3)
    pass_on(1, 0)
    for d in order:
        pass_on(1, d)
    swap(1, 1)
    swap(1, 3)
    for cp in far[:8]:
        cp.wait_recv()
    swap(0, 2)
    for cp in far[8:]:
        cp.wait_recv()
    swap(1, 2)
    for cp in swaps:
        cp.wait_recv()
    for cp in net.sent:
        cp.wait_send()


def flush(*refs):
    n = len(refs) // 2
    sems = refs[2 * n]
    cps = [pltpu.make_async_copy(refs[i], refs[n + i], sems.at[i]) for i in range(n)]
    for cp in cps:
        cp.start()
    for cp in cps:
        cp.wait()


def local(grad_parts, adam_m, adam_v, params_inner, snapshot, momentum):
    vmem = pl.BlockSpec(memory_space=pltpu.VMEM)
    hbm = pl.BlockSpec(memory_space=pl.ANY)
    V = pltpu.VMEM
    args = (
        grad_parts.reshape(4, 4, 16, D),
        adam_m[0],
        adam_v[0],
        params_inner[0],
        snapshot,
        momentum,
    )
    outs = pl.pallas_call(
        kernel,
        out_shape=(
            jax.ShapeDtypeStruct((4, D), F32),
            jax.ShapeDtypeStruct((4, D), F32),
            jax.ShapeDtypeStruct((4, 2048), F32),
            jax.ShapeDtypeStruct((4, 2048), F32),
            jax.ShapeDtypeStruct((4, 4, 16, D), BF16),
        ),
        in_specs=[pl.BlockSpec(memory_space=pltpu.HBM)] * 6,
        out_specs=(vmem, vmem, vmem, vmem, hbm),
        scratch_shapes=[
            V((4, D), F32),
            V((4, D), F32),
            V((4, D), F32),
            V((4, D), F32),
            V((4, D), F32),
            V((4, 4, 16, D), BF16),
            [V((2, 3, 2, 16, w), BF16) for w in WS],
            [V((2, 3, 2, 4, 16, w), BF16) for w in CWS],
            [V((2, 2, 16, w), BF16) for w in WS],
            [V((2, 2, 4, 16, w), BF16) for w in CWS],
            [V((4, 16, w), BF16) for w in WS],
            [V((4, 4, 16, w), BF16) for w in CWS],
            [V((2, 2, 3, 2, 16, w), BF16) for w in CWS],
            [V((2, 2, 2, 16, w), BF16) for w in CWS],
            [V((4, 4, 16, 256), BF16), V((4, 4, 32, 128), BF16)],
            [V((4, 4, 16, 256), BF16), V((4, 4, 32, 128), BF16)],
            V((3, 4, 16, ZW), BF16),
            V((4, 16, ZW), BF16),
            V((3, 16, ZW), BF16),
            V((4, 16, ZW // 4), BF16),
            V((3, 16, ZW // 4), BF16),
            V((4, D), F32),
            V((2, 8, 128), F32),
            V((16, 8, 128), F32),
            V((2, 4, 8, 128), F32),
            V((4, 4, 16, 128), BF16),
            V((4, 4, 16, 128), BF16),
            V((4, 4, 16, 128), BF16),
            V((4, 2, 16, 128), F32),
            V((4, 2, 16, 128), F32),
            V((2, 16, 256), BF16),
            pltpu.SemaphoreType.DMA((NSEM,)),
            pltpu.SemaphoreType.DMA((NSEM,)),
            pltpu.SemaphoreType.DMA((NR + 5,)),
            pltpu.SemaphoreType.REGULAR((4,)),
        ],
        compiler_params=pltpu.CompilerParams(
            collective_id=0, has_side_effects=True, vmem_limit_bytes=40 * 2**20
        ),
        name="outer_step",
    )(*[pltpu.with_memory_space_constraint(a, pltpu.HBM) for a in args])
    m, v, pn, mn, w = pl.pallas_call(
        flush,
        out_shape=tuple(jax.ShapeDtypeStruct(o.shape, o.dtype) for o in outs),
        in_specs=[hbm] * 5,
        out_specs=(hbm,) * 5,
        scratch_shapes=[pltpu.SemaphoreType.DMA((5,))],
        compiler_params=pltpu.CompilerParams(vmem_limit_bytes=2**20),
        name="write_out",
    )(*outs)
    return m[None], v[None], pn, mn, w.reshape(256, D)


def solution(mesh):
    rows = P("rep", "fsdp", None)
    flat = P("fsdp", None)
    return jax.shard_map(
        local,
        mesh=mesh,
        in_specs=(rows, rows, rows, rows, flat, flat),
        out_specs=(rows, rows, P("fsdp", "rep"), P("fsdp", "rep"), P()),
        check_vma=False,
    )
```

```python
import functools

import jax
import jax.numpy as jnp
from jax import lax
from jax.experimental import pallas as pl
from jax.experimental.pallas import tpu as pltpu
from jax.sharding import PartitionSpec as P

D = 8192
K = 2
PIECE = (256, 128)
NR = 2 * K
WS = (2048, 1536)
CWS = tuple(w // 4 for w in WS)
ZO = 2 * sum(WS)
ZW = D - ZO
NSEM = 260
F32 = jnp.float32
BF16 = jnp.bfloat16


def mo(v, m=128):
    return pl.multiple_of(v, m)


class Ring:
    def __init__(self, net, i, to_next, to_prev, raw, own, land, acc):
        self.net, self.i = net, i
        self.to_next, self.to_prev = to_next, to_prev
        self.raw, self.own, self.land, self.acc = raw, own, land, acc

    def start(self):
        self.start_far()
        self.start_near()

    def start_far(self):
        i, net = self.i, self.net
        far = (i + 2) % 4
        self.a = [
            net.send(self.raw(far, 0), self.land.at[0, 0], self.to_next),
            net.send(self.raw(far, 1), self.land.at[1, 0], self.to_prev),
        ]

    def leave(self, copies):
        for cp in copies:
            cp.wait_send()
            self.net.sent = [other for other in self.net.sent if other is not cp]

    def start_near(self):
        i, net = self.i, self.net
        nxt, prv = (i + 1) % 4, (i + 3) % 4
        self.b = [
            net.send(self.raw(nxt, 1), self.land.at[0, 1], self.to_next),
            net.send(self.raw(prv, 0), self.land.at[1, 1], self.to_prev),
        ]

    def forward(self):
        i, net = self.i, self.net
        nxt, prv = (i + 1) % 4, (i + 3) % 4
        self.a[0].wait_recv()
        add(self.acc.at[0], [self.own(nxt, 0), self.land.at[0, 0]])
        c0 = net.send(self.acc.at[0], self.land.at[0, 2], self.to_next)
        self.a[1].wait_recv()
        add(self.acc.at[1], [self.own(prv, 1), self.land.at[1, 0]])
        c1 = net.send(self.acc.at[1], self.land.at[1, 2], self.to_prev)
        self.c = [c0, c1]

    def wait(self):
        for cp in self.b + self.c:
            cp.wait_recv()

    def terms(self, hh):
        land = self.land
        if hh == 0:
            return [self.own(self.i, 0), land.at[0, 2], land.at[1, 1]]
        return [self.own(self.i, 1), land.at[0, 1], land.at[1, 2]]


class Direct(Ring):
    def __init__(self, net, i, to, raw, land):
        self.net, self.i, self.to, self.own, self.land = net, i, to, raw, land

    def start(self):
        self.b = [
            self.net.send(self.own((self.i + d) % 4, hh), self.land.at[hh, d - 1], self.to[d - 1])
            for d in (2, 1, 3)
            for hh in range(2)
        ]
        self.c = []

    def forward(self):
        pass

    def terms(self, hh):
        return [self.own(self.i, hh)] + [self.land.at[hh, d] for d in range(3)]


def add(dst, srcs):
    shape = dst.shape
    if len(shape) == 4:

        def body(j, _):
            dst[:, j] = functools.reduce(
                jnp.add, [s[:, j].astype(F32) for s in srcs]
            ).astype(BF16)
            return 0

        lax.fori_loop(0, shape[1], body, 0)
    else:

        def body(j, _):
            at = pl.ds(mo(j * step, step), step)
            dst[:, :, at] = functools.reduce(
                jnp.add, [s[:, :, at].astype(F32) for s in srcs]
            ).astype(BF16)
            return 0

        step = 512 if shape[2] % 512 == 0 else shape[2]
        lax.fori_loop(0, shape[2] // step, body, 0)


class Net:
    def __init__(self, ss, rs):
        self.ss, self.rs, self.n = ss, rs, 0
        self.sent = []

    def send(self, src, dst, dev):
        n = self.n
        self.n += 1
        assert n < NSEM
        cp = pltpu.make_async_remote_copy(
            src, dst, self.ss.at[n], self.rs.at[n], device_id=dev
        )
        cp.start()
        self.sent.append(cp)
        return cp


def offsets(yy):
    return [p * 1024 + yy * 256 + t * 128 for p in range(2) for t in range(2)]


def rows4(v, b):
    return v[4 * b : 4 * b + 4]


def kernel(
    grad, m_in, v_in, p_in, snap_in, mom_in,
    m_out, v_out, pn_out, mn_out, w_out,
    m_ref, v_ref, p_ref, snap, mom, G, LX1, LY1, AX1, AY1, SX1, SY1, L2, A2, M3, R3, LC1, SC, LC2, MC, RC, Gs, PK, P1, P2, Pq, E, X, SM, SX, Wb,
    ss, rs, ls, bs,
):
    rep, f = lax.axis_index("rep"), lax.axis_index("fsdp")
    h, c = rep // 2, rep % 2
    z, x, y = f // 16, (f // 4) % 4, f % 4
    zp = z + 1 - 2 * (z % 2)
    Z = 4 * h + z

    def dev(h=h, c=c, z=z, x=x, y=y):
        return (2 * h + c, 16 * z + 4 * x + y)

    loc = []
    for r in range(NR):
        at = pl.ds(r * 2048, 2048)
        cp = pltpu.make_async_copy(grad.at[:, :, :, at], G.at[:, :, :, at], ls.at[r])
        cp.start()
        loc.append(cp)

    held = []
    for n, (src, dst) in enumerate(
        ((m_in, m_ref), (v_in, v_ref), (p_in, p_ref), (snap_in, snap), (mom_in, mom))
    ):
        cp = pltpu.make_async_copy(src, dst, ls.at[NR + n])
        cp.start()
        held.append(cp)

    xn, xp = dev(x=(x + 1) % 4), dev(x=(x + 3) % 4)
    yn, yp = dev(y=(y + 1) % 4), dev(y=(y + 3) % 4)
    sib = dev(c=1 - c)
    Zn, Zp = (Z + 1) % 8, (Z + 7) % 8
    line = [dev(h=Zn // 4, z=Zn % 4), dev(h=Zp // 4, z=Zp % 4), sib]
    bar = pltpu.get_barrier_semaphore()
    for d in [xn, xp, yn, yp] + line:
        pl.semaphore_signal(bar, 1, device_id=d)
    pl.semaphore_wait(bar, 7)

    def ahead(n):
        for d in line:
            pl.semaphore_signal(bs.at[n], 1, device_id=d)
        pl.semaphore_wait(bs.at[n], 3)

    net = Net(ss, rs)

    def origin(k, s):
        return 2 * sum(WS[:k]) + s * WS[k]

    def first(r):
        k = r // 2
        o, w, cw = origin(k, r % 2), WS[k], CWS[k]
        if r % 2 == 0:

            def chunk(src, j, hh):
                return src.at[pl.ds(2 * hh, 2), j, :, pl.ds(o, w)]

            return Ring(
                net, x, xn, xp, functools.partial(chunk, grad), functools.partial(chunk, G),
                LX1[k], AX1[k],
            )

        def chunk(src, j, hh):
            return src.at[pl.ds(2 * hh, 2), :, :, pl.ds(mo(o + j * cw), cw)]

        return Ring(
            net, y, yn, yp, functools.partial(chunk, grad), functools.partial(chunk, G),
            LY1[k], AY1[k],
        )

    def second(r):
        k = r // 2
        if r % 2 == 0:

            def chunk(j, hh):
                return SX1[k].at[pl.ds(2 * hh, 2), :, pl.ds(mo(j * CWS[k]), CWS[k])]

            if k == K - 1:
                to = [dev(y=(y + d) % 4) for d in (1, 2, 3)]
                return Direct(net, y, to, chunk, L2[k].at[r % 2])
            return Ring(net, y, yn, yp, chunk, chunk, L2[k].at[r % 2], A2[k].at[r % 2])

        def chunk(j, hh):
            return SY1[k].at[pl.ds(2 * hh, 2), j]

        if k == K - 1:
            to = [dev(x=(x + d) % 4) for d in (1, 2, 3)]
            return Direct(net, x, to, chunk, L2[k].at[r % 2])
        return Ring(net, x, xn, xp, chunk, chunk, L2[k].at[r % 2], A2[k].at[r % 2])

    one = [first(r) for r in range(NR)]
    two = [second(r) for r in range(NR)]

    def finish_first(k):
        for r in (2 * k, 2 * k + 1):
            one[r].wait()
            dst = (SX1 if r % 2 == 0 else SY1)[k]
            for hh in range(2):
                add(dst.at[pl.ds(2 * hh, 2)], one[r].terms(hh))
        for r in (2 * k, 2 * k + 1):
            two[r].start()

    def finish_second(k):
        rings = two[2 * k], two[2 * k + 1]
        for ring in rings:
            ring.wait()
        for zz in range(4):
            pieces = []
            for ring in rings:
                s = functools.reduce(
                    jnp.add, [t[zz % 2].astype(F32) for t in ring.terms(zz // 2)]
                )
                pw = PIECE[k]
                pieces += [s[:, o : o + pw] for o in range(0, CWS[k], pw)]
            while len(pieces) % 4:
                pieces.append(jnp.zeros_like(pieces[0]))
            for yy in range(4):
                M3[k][zz, yy] = jnp.concatenate([rows4(s, yy) for s in pieces], 0).astype(BF16)
        return [
            net.send(
                M3[k].at[(z + dz) % 4, (y + dy) % 4],
                R3[k].at[dz, dy],
                dev(z=(z + dz) % 4, y=(y + dy) % 4),
            )
            for dz in (2, 1, 3, 0)
            for dy in (2, 1, 3, 0)
            if dz or dy
        ]

    one[0].start_far()
    one[1].start_far()
    ahead(0)
    ahead(1)
    one[0].leave(one[0].a + one[1].a)
    one[0].start_near()
    one[1].start_near()
    one[2].start_far()
    one[3].start_far()
    ahead(2)
    ahead(3)
    zcols = pl.ds(ZO, ZW)
    zfirst = [
        net.send(grad.at[(z + d) % 4, :, :, zcols], LC1.at[d - 1], dev(z=(z + d) % 4))
        for d in (2, 1, 3)
    ]
    for cp in loc:
        cp.wait()
    one[0].forward()
    one[1].forward()
    one[0].leave(one[0].c + one[1].c)
    one[2].start_near()
    one[3].start_near()
    finish_first(0)
    one[2].forward()
    one[3].forward()
    two[0].forward()
    two[1].forward()
    finish_first(1)
    for cp in zfirst:
        cp.wait_recv()
    add(SC, [G.at[z, :, :, zcols]] + [LC1.at[d] for d in range(3)])
    zsecond = [
        net.send(SC.at[(x + d) % 4], LC2.at[d - 1], dev(x=(x + d) % 4)) for d in (2, 1, 3)
    ]
    early = finish_second(0)
    for cp in held:
        cp.wait()
    for n, ref in enumerate((snap, mom)):
        for yy in range(4):
            SM[yy, n] = jnp.concatenate(
                [ref[:, pl.ds(mo(rep * 2048 + o), 128)] for o in offsets(yy)], 0
            )
    sm = [net.send(SM.at[(y + d) % 4], SX.at[y], dev(y=(y + d) % 4)) for d in (2, 1, 3)]
    SX[y] = SM[y]
    two[2].forward()
    two[3].forward()
    third = finish_second(1)
    for cp in zsecond:
        cp.wait_recv()
    s = SC[x].astype(F32)
    for d in range(3):
        s = s + LC2[d].astype(F32)
    for yy in range(4):
        MC[yy] = jnp.concatenate(
            [rows4(s[:, t * ZW // 4 : (t + 1) * ZW // 4], yy) for t in range(4)], 0
        ).astype(BF16)
    third += [
        net.send(MC.at[(y + d) % 4], RC.at[d - 1], dev(y=(y + d) % 4)) for d in (2, 1, 3)
    ]

    def collect(k):
        for dy in range(4):
            g = None
            for dz in range(4):
                t = (R3[k][dz, dy] if dz or dy else M3[k][z, y]).astype(F32)
                g = t if g is None else g + t
            ys = (y + 4 - dy) % 4
            pw = PIECE[k]
            n = CWS[k] // pw
            for s in range(2):
                for t in range(n):
                    at = pl.ds(mo(origin(k, s) + ys * CWS[k] + t * pw), pw)
                    Gs[:, at] = rows4(g, n * s + t)
    def adam(q, top):
        parts = []
        for t in range(4):
            at = pl.ds(q * 2048 + t * 512, 512)
            g, params = Gs[:, at], p_ref[:, at]
            m_next = 0.9 * m_ref[:, at] + 0.1 * g
            v_next = 0.95 * v_ref[:, at] + 0.05 * g * g
            m_out[:, at] = m_next
            v_out[:, at] = v_next
            inner = params - 0.02 * (m_next / (jnp.sqrt(v_next) + 1e-8) + 0.1 * params)
            pseudo = snap[:, at] - inner
            parts.append(pseudo)
            size = jnp.abs(pseudo)
            top = size if top is None else jnp.maximum(top, size)
        wide = jnp.concatenate(parts, 1)
        for yy in range(4):
            Pq[q, yy] = jnp.concatenate([wide[:, o : o + 128] for o in offsets(yy)], 0).astype(BF16)
        return top

    for cp in early:
        cp.wait_recv()
    collect(0)
    top = adam(1, adam(0, None))
    for cp in third:
        cp.wait_recv()
    collect(1)
    g = MC[y].astype(F32)
    for d in range(3):
        g = g + RC[d].astype(F32)
    for t in range(4):
        Gs[:, ZO + t * ZW // 4 : ZO + (t + 1) * ZW // 4] = rows4(g, t)
    top = adam(3, adam(2, top))
    tile = functools.reduce(jnp.maximum, [top[:, 128 * i : 128 * i + 128] for i in range(4)])
    PK[0] = jnp.concatenate([tile, tile], 0)

    got = [
        net.send(PK.at[0], P1.at[4 * a + b], dev(x=(x + a) % 4, y=(y + b) % 4))
        for a in (2, 1, 3, 0)
        for b in (2, 1, 3, 0)
        if a or b
    ]

    def flip(dr):
        return (1 - h if dr // 2 else h), (1 - c if dr % 2 else c)

    sent_e = []
    for dr in (3, 2, 1, 0):
        h2, c2 = flip(dr)
        for d in (2, 1, 3, 0):
            if dr or d:
                to = (y + d) % 4
                sent_e.append(net.send(Pq.at[2 * h2 + c2, to], X.at[dr, y], dev(h=h2, c=c2, y=to)))
    peak = PK[0]
    for cp in got:
        cp.wait_recv()
    for i in range(1, 16):
        peak = jnp.maximum(peak, P1[i])
    PK[1] = peak
    got = []
    for dr in (3, 2, 1, 0):
        h2, c2 = flip(dr)
        for e in (1, 0):
            if dr or e:
                got.append(
                    net.send(PK.at[1], P2.at[e, dr], dev(h=h2, c=c2, z=zp if e else z))
                )
    for cp in sm + sent_e:
        cp.wait_recv()
    for cp in got:
        cp.wait_recv()
    factors = []
    for dr in range(4):
        high = jnp.maximum(P2[0, dr] if dr else peak, P2[1, dr])
        high = jnp.max(high, axis=(0, 1), keepdims=True)
        factors.append(0.5 / jnp.maximum(high, 0.5))
    X[0, y] = Pq[rep, y]
    new = []
    for ys in range(4):
        terms = [X[dr, ys].astype(F32) * factors[dr] for dr in range(4)]
        avg = functools.reduce(jnp.add, terms) / 4
        new.append(SX[ys, 0] - 0.7 * (avg + 0.9 * (0.9 * SX[ys, 1] + avg)))
    for p in range(2):
        for t in range(2):
            Wb[p, :, pl.ds(t * 128, 128)] = jnp.concatenate(
                [rows4(v, 2 * p + t) for v in new], 0
            ).astype(BF16)

    def small(p):
        return w_out.at[z, x, :, pl.ds(mo((2 * h + c) * 2048 + p * 1024 + y * 256), 256)]

    for p in range(2):
        cp = pltpu.make_async_copy(Wb.at[p], small(p), ls.at[p])
        cp.start()
        loc[p] = cp
    strips = [[], []]
    for s in range(2):
        for d in (2, 1, 3, 0):
            if s or d:
                for p in range(2):
                    to = dev(h=1 - h if s else h, z=(z + d) % 4)
                    strips[s].append(net.send(Wb.at[p], small(p), to))

    wide_e = []
    for dr in (3, 2, 1):
        h2, c2 = flip(dr)
        wide_e.append(net.send(Pq.at[2 * h2 + c2], E.at[dr], dev(h=h2, c=c2)))

    def part(p, s, mid, last):
        q = 2 * (1 - h if s else h) + c
        if p == 0:
            return w_out.at[:, last, :, pl.ds(mo(q * 2048 + mid * 256), 256)]
        return w_out.at[:, mid, :, pl.ds(mo(q * 2048 + 1024 + last * 256), 256)]

    def large(p, s, last):
        q = 2 * (1 - h if s else h) + c
        if p == 0:
            return w_out.at[:, last, :, pl.ds(mo(q * 2048), 1024)]
        return w_out.at[:, :, :, pl.ds(mo(q * 2048 + 1024 + last * 256), 256)]

    ways = ((y, x, xn, xp), (x, y, yn, yp))
    mids, near, far, swaps = {}, {}, [], []

    def send_mid(s):
        for d in (2, 1, 3):
            for p, (m, la, _, _) in enumerate(ways):
                to = dev(y=(y + d) % 4) if p == 0 else dev(x=(x + d) % 4)
                mids[p, s, d] = net.send(part(p, s, m, la), part(p, s, m, la), to)

    def send_last(s, d):
        for p, (m, la, nx, pv) in enumerate(ways):
            if d:
                mids[p, s, d].wait_recv()
            blk = part(p, s, (m + 4 - d) % 4, la)
            near[p, s, d] = net.send(blk, blk, nx), net.send(blk, blk, pv)

    def pass_on(s, d):
        for p, (m, la, nx, pv) in enumerate(ways):
            mid = (m + 4 - d) % 4
            from_prev, from_next = near[p, s, d]
            if d % 2 == 0:
                from_prev.wait_recv()
                blk = part(p, s, mid, (la + 3) % 4)
                far.append(net.send(blk, blk, nx))
                from_next.wait_recv()
            else:
                from_next.wait_recv()
                blk = part(p, s, mid, (la + 1) % 4)
                far.append(net.send(blk, blk, pv))
                from_prev.wait_recv()

    def swap(s, d):
        for p, (m, la, nx, pv) in enumerate(ways):
            blk = large(p, s, (la + 4 - d) % 4)
            swaps.append(net.send(blk, blk, sib))

    for p in range(2):
        loc[p].wait()
    for s in range(2):
        for cp in strips[s]:
            cp.wait_recv()
        send_mid(s)
        send_last(s, 0)

    order = (1, 3, 2)
    for d in order:
        send_last(0, d)
    swap(0, 0)
    pass_on(0, 0)
    for d in order:
        send_last(1, d)
    swap(1, 0)
    for cp in wide_e:
        cp.wait_recv()
    for yy in range(4):
        terms = [
            (E[dr, yy] if dr else Pq[rep, yy]).astype(F32) * factors[dr] for dr in range(4)
        ]
        averaged = functools.reduce(jnp.add, terms) / 4
        m_new = 0.9 * SM[yy, 1] + averaged
        p_new = SM[yy, 0] - 0.7 * (averaged + 0.9 * m_new)
        for b, o in enumerate(offsets(yy)):
            mn_out[:, o : o + 128] = rows4(m_new, b)
            pn_out[:, o : o + 128] = rows4(p_new, b)

    for d in order:
        pass_on(0, d)
    swap(0, 1)
    swap(0, 3)
    pass_on(1, 0)
    for d in order:
        pass_on(1, d)
    swap(1, 1)
    swap(1, 3)
    for cp in far[:8]:
        cp.wait_recv()
    swap(0, 2)
    for cp in far[8:]:
        cp.wait_recv()
    swap(1, 2)
    for cp in swaps:
        cp.wait_recv()
    for cp in net.sent:
        cp.wait_send()


def flush(*refs):
    n = len(refs) // 2
    sems = refs[2 * n]
    cps = [pltpu.make_async_copy(refs[i], refs[n + i], sems.at[i]) for i in range(n)]
    for cp in cps:
        cp.start()
    for cp in cps:
        cp.wait()


def local(grad_parts, adam_m, adam_v, params_inner, snapshot, momentum):
    vmem = pl.BlockSpec(memory_space=pltpu.VMEM)
    hbm = pl.BlockSpec(memory_space=pl.ANY)
    V = pltpu.VMEM
    args = (
        grad_parts.reshape(4, 4, 16, D),
        adam_m[0],
        adam_v[0],
        params_inner[0],
        snapshot,
        momentum,
    )
    outs = pl.pallas_call(
        kernel,
        out_shape=(
            jax.ShapeDtypeStruct((4, D), F32),
            jax.ShapeDtypeStruct((4, D), F32),
            jax.ShapeDtypeStruct((4, 2048), F32),
            jax.ShapeDtypeStruct((4, 2048), F32),
            jax.ShapeDtypeStruct((4, 4, 16, D), BF16),
        ),
        in_specs=[pl.BlockSpec(memory_space=pltpu.HBM)] * 6,
        out_specs=(vmem, vmem, vmem, vmem, hbm),
        scratch_shapes=[
            V((4, D), F32),
            V((4, D), F32),
            V((4, D), F32),
            V((4, D), F32),
            V((4, D), F32),
            V((4, 4, 16, D), BF16),
            [V((2, 3, 2, 16, w), BF16) for w in WS],
            [V((2, 3, 2, 4, 16, w), BF16) for w in CWS],
            [V((2, 2, 16, w), BF16) for w in WS],
            [V((2, 2, 4, 16, w), BF16) for w in CWS],
            [V((4, 16, w), BF16) for w in WS],
            [V((4, 4, 16, w), BF16) for w in CWS],
            [V((2, 2, 3, 2, 16, w), BF16) for w in CWS],
            [V((2, 2, 2, 16, w), BF16) for w in CWS],
            [V((4, 4, 16, 256), BF16), V((4, 4, 32, 128), BF16)],
            [V((4, 4, 16, 256), BF16), V((4, 4, 32, 128), BF16)],
            V((3, 4, 16, ZW), BF16),
            V((4, 16, ZW), BF16),
            V((3, 16, ZW), BF16),
            V((4, 16, ZW // 4), BF16),
            V((3, 16, ZW // 4), BF16),
            V((4, D), F32),
            V((2, 8, 128), F32),
            V((16, 8, 128), F32),
            V((2, 4, 8, 128), F32),
            V((4, 4, 16, 128), BF16),
            V((4, 4, 16, 128), BF16),
            V((4, 4, 16, 128), BF16),
            V((4, 2, 16, 128), F32),
            V((4, 2, 16, 128), F32),
            V((2, 16, 256), BF16),
            pltpu.SemaphoreType.DMA((NSEM,)),
            pltpu.SemaphoreType.DMA((NSEM,)),
            pltpu.SemaphoreType.DMA((NR + 5,)),
            pltpu.SemaphoreType.REGULAR((4,)),
        ],
        compiler_params=pltpu.CompilerParams(
            collective_id=0, has_side_effects=True, vmem_limit_bytes=40 * 2**20
        ),
        name="outer_step",
    )(*[pltpu.with_memory_space_constraint(a, pltpu.HBM) for a in args])
    m, v, pn, mn, w = pl.pallas_call(
        flush,
        out_shape=tuple(jax.ShapeDtypeStruct(o.shape, o.dtype) for o in outs),
        in_specs=[hbm] * 5,
        out_specs=(hbm,) * 5,
        scratch_shapes=[pltpu.SemaphoreType.DMA((5,))],
        compiler_params=pltpu.CompilerParams(vmem_limit_bytes=2**20),
        name="write_out",
    )(*outs)
    return m[None], v[None], pn, mn, w.reshape(256, D)


def solution(mesh):
    rows = P("rep", "fsdp", None)
    flat = P("fsdp", None)
    return jax.shard_map(
        local,
        mesh=mesh,
        in_specs=(rows, rows, rows, rows, flat, flat),
        out_specs=(rows, rows, P("fsdp", "rep"), P("fsdp", "rep"), P()),
        check_vma=False,
    )
```
